256 devices in a mesh: dp: 16 (over x, y), replica: 16 (over z, core).
Axes of the slice: x: 4, y: 4, z: 8, core: 2. Of those that a mesh axis runs over, the one named last changes fastest.
Arguments:
- picture_probes: bfloat16 [8192, 32, 256], P(('dp', 'replica')), may hold values from -2 to 2
- caption_vectors: bfloat16 [8192, 256], P(('dp', 'replica')), may hold values from -2 to 2
- chosen_slot_per_match: int32 [8192, 8192], P(('dp', 'replica')), may hold values from 0 to 31
- softmax_heat: float32 [1], replicated, may hold values from 0.05 to 0.1
Outputs:
- query_grads: float32 [8192, 32, 256], P(('dp', 'replica'))
- text_grads: float32 [8192, 256], P(('dp', 'replica'))
The draws below stay inside these ranges and needn't reach their ends.
All inputs are finite; a program needn't handle non-finite values.
Results may differ from the reference program's by a relative error of at most 0.00105.
The reference program's roundings to bfloat16 on the way count: a program that leaves them out, or rounds other values in their place, can miss the bound.
Values may be sent and summed in bfloat16 or wider, within the bound.
No kernel may reach another device: no remote copies, remote signals or barrier semaphores. Data moves between devices by JAX's collectives and lax.ppermute only.
A program may use at most 64 MiB of HBM per device.

```python
import math
import jax
import jax.numpy as jnp
import numpy as np
from jax import lax

QUERIES = 32
WIDTH = 256
PAIRS = 8192


def common_pieces(key):
    lookup_vector, key_dir, key_perm = jax.random.split(key, 3)
    vectors = jax.random.truncated_normal(lookup_vector, -6.0, 6.0, (PAIRS, WIDTH), jnp.float32) / WIDTH ** 0.5
    direction = jax.random.rademacher(key_dir, (WIDTH,), dtype=jnp.float32) / WIDTH ** 0.5
    partner = jax.random.permutation(key_perm, PAIRS)
    return (vectors, direction, partner)


def draw_picture_probes(key, part):
    vectors, direction, partner = common_pieces(key)
    key = jax.random.fold_in(key, 11)
    noise_key, slot_key = jax.random.split(key)
    slot_direction = jax.random.truncated_normal(slot_key, -4.0, 4.0, (QUERIES, WIDTH), jnp.float32) / WIDTH ** 0.5
    noise = jax.random.truncated_normal(noise_key, -6.0, 6.0, (PAIRS, QUERIES, WIDTH), jnp.float32) / WIDTH ** 0.5
    image_weight = 0.35
    shared_weight = 0.5
    own_weight = 0.8
    values = image_weight * vectors[:, None, :] + shared_weight * slot_direction[None, :, :] + own_weight * noise
    return values.astype(jnp.bfloat16)


def draw_caption_vectors(key, part):
    vectors, direction, partner = common_pieces(key)
    key = jax.random.fold_in(key, 23)
    noise = jax.random.truncated_normal(key, -6.0, 6.0, (PAIRS, WIDTH), jnp.float32) / WIDTH ** 0.5
    lift = 0.3
    values = 0.6 * vectors + 0.6 * vectors[partner] + 0.5 * noise + lift * direction[None, :]
    return values.astype(jnp.bfloat16)


def place_ends(entries, key, low, top_value):
    shape = entries.shape
    spot = [jax.random.randint(jax.random.fold_in(key, axis), (), 0, shape[axis]) for axis in range(len(shape))]
    entries = entries.at[tuple(spot)].set(low)
    longest = shape.index(max(shape))
    spot[longest] = (spot[longest] + 1) % shape[longest]
    return entries.at[tuple(spot)].set(top_value)


def rank_table(number_of, lean):
    weights = [(1 << 20) // math.isqrt(standing ** lean) + 1 for standing in range(1, number_of + 1)]
    deviation = 1 + sum(weights) // (1 << 30)
    return np.cumsum(np.array([max(1, weight // deviation) for weight in weights]))


def skewed_ids(rng, extent, count, lean):
    table = rank_table(count, lean)
    pick = jax.random.randint(jax.random.fold_in(rng, 1), extent, 0, int(table[count - 1]))
    rank = jnp.searchsorted(jnp.asarray(table, jnp.int32), pick, side="right")
    return jax.random.permutation(jax.random.fold_in(rng, 2), count)[rank].astype(jnp.int32)


def setup_inputs(seed: int = 0) -> dict:
    splits = jax.random.split(jax.random.key(seed), 5)
    picture_probes = draw_picture_probes(jax.random.fold_in(splits[4], 71), 0)
    caption_vectors = draw_caption_vectors(jax.random.fold_in(splits[4], 71), 0)
    chosen_slot_per_match = place_ends(skewed_ids(splits[2], (PAIRS, PAIRS), QUERIES, 2), jax.random.fold_in(splits[2], 3), 0, QUERIES - 1).astype(jnp.int32)
    softmax_heat = jnp.clip(jnp.exp(jax.random.uniform(splits[3], (1,), jnp.float32, math.log(0.05), math.log(0.1))), 0.05, 0.1)
    return {"picture_probes": picture_probes, "caption_vectors": caption_vectors, "chosen_slot_per_match": chosen_slot_per_match, "softmax_heat": softmax_heat}


EPS = 1e-06

def pick_query(dense, index):
    levels = jnp.arange(dense.shape[1], dtype=jnp.int32)
    hit = index[:, None, :] == levels[None, :, None]
    return lax.optimization_barrier(jnp.sum(jnp.where(hit, dense, 0.0), axis=1))

def normalized_rows(values):
    wide = values.astype(jnp.float32)
    scale = lax.rsqrt(lax.optimization_barrier(jnp.sum(wide * wide, axis=-1, keepdims=True)) + EPS)
    return (wide * scale, scale)

def reference(picture_probes, caption_vectors, chosen_slot_per_match, softmax_heat):
    pairs, count, width = picture_probes.shape
    query_normalized, q_scale = normalized_rows(picture_probes)
    t_unit, t_scale = normalized_rows(caption_vectors)
    q_half = query_normalized.astype(jnp.bfloat16)
    text_halved = t_unit.astype(jnp.bfloat16)
    text_broadened = text_halved.astype(jnp.float32)
    reciprocal_length = 1.0 / softmax_heat[0]
    block = math.gcd(pairs, 64)
    nblocks = pairs // block
    q_blocks = q_half.reshape(nblocks, block, count, width)
    fwd_blocks = chosen_slot_per_match.reshape(nblocks, block, pairs)

    def scores(args):
        q_piece, fwd = args
        dense = jnp.einsum('iqd,jd->iqj', q_piece.astype(jnp.float32), text_broadened)
        return pick_query(dense, fwd)
    s_one = lax.map(scores, (q_blocks, fwd_blocks)).reshape(pairs, pairs)
    e_one = jnp.exp(s_one * reciprocal_length)
    p_one = e_one / lax.optimization_barrier(jnp.sum(e_one, axis=1, keepdims=True))
    p_two = e_one / lax.optimization_barrier(jnp.sum(e_one, axis=0, keepdims=True))
    target = 0.9 * jnp.eye(pairs, dtype=jnp.float32) + 0.1 / pairs
    g_one = (p_one - target) * (0.5 * reciprocal_length)
    g_two = (p_two - target) * (0.5 * reciprocal_length)
    g_both = (g_one + g_two).reshape(nblocks, block, pairs)
    levels = jnp.arange(count, dtype=jnp.int32)

    def backward(dt_acc, args):
        q_piece, fwd, gradient_pair = args
        mix = jnp.where(fwd[:, None, :] == levels[None, :, None], gradient_pair[:, None, :], 0.0)
        mix = lax.optimization_barrier(mix.astype(jnp.bfloat16)).astype(jnp.float32)
        dq_piece = jnp.einsum('iqj,jd->iqd', mix, text_broadened)
        dt_acc = dt_acc + jnp.einsum('iqj,iqd->jd', mix, q_piece.astype(jnp.float32))
        return (dt_acc, dq_piece)
    dt_half, dq_half = lax.scan(backward, jnp.zeros((pairs, width), jnp.float32), (q_blocks, fwd_blocks, g_both))
    dq_half = dq_half.reshape(pairs, count, width)
    query_grads = (dq_half - query_normalized * lax.optimization_barrier(jnp.sum(query_normalized * dq_half, axis=-1, keepdims=True))) * q_scale
    text_grads = (dt_half - t_unit * lax.optimization_barrier(jnp.sum(t_unit * dt_half, axis=-1, keepdims=True))) * t_scale
    return (query_grads, text_grads)
```

```python
import jax
import jax.numpy as jnp
from jax import lax
from jax.experimental import pallas as pl
from jax.experimental.pallas import tpu as pltpu
from jax.sharding import Mesh
from jax.sharding import PartitionSpec as P

EPS = 1e-06
VMEM_LIMIT = 56 * 1024 * 1024
SWAP = [(0, 1), (1, 0)]


def normalized_rows(values):
    wide = values.astype(jnp.float32)
    scale = lax.rsqrt(jnp.sum(wide * wide, axis=-1, keepdims=True) + EPS)
    return (wide * scale, scale)


def spread(values, axis):
    count = lax.axis_size(axis)
    return lax.all_to_all(jnp.broadcast_to(values[None], (count, *values.shape)), axis, 0, 0, tiled=True)


def gather_members(near_ref, far_ref, query):
    return jnp.concatenate(
        [near_ref[0, query], near_ref[1, query], far_ref[0, query], far_ref[1, query]], axis=0
    )


def score_kernel(heat_ref, near_ref, far_ref, text_ref, slot_ref, e_ref, row_ref, column_ref):
    step = pl.program_id(0)
    count = near_ref.shape[1]
    images = e_ref.shape[0]
    group = 4
    slots = slot_ref[...].astype(jnp.float32)
    texts = text_ref[...]
    picked = jnp.zeros(e_ref.shape, jnp.float32)
    for first in range(0, count, group):
        queries = jnp.concatenate(
            [gather_members(near_ref, far_ref, first + k) for k in range(group)], axis=0
        )
        dense = lax.dot_general(
            queries, texts, (((1,), (1,)), ((), ())), preferred_element_type=jnp.float32
        )
        for k in range(group):
            picked = jnp.where(slots == float(first + k), dense[k * images : (k + 1) * images], picked)
    e = jnp.exp(picked * (1.0 / heat_ref[0]))
    e_ref[...] = e
    column_ref[...] = jnp.sum(e, axis=0, keepdims=True)

    @pl.when(step == 0)
    def _():
        row_ref[...] = jnp.zeros_like(row_ref)

    row_ref[...] += jnp.sum(e, axis=1, keepdims=True)


def grad_kernel(
    total,
    heat_ref,
    first_ref,
    near_ref,
    far_ref,
    text_ref,
    slot_ref,
    e_ref,
    row_ref,
    column_ref,
    dq_near_ref,
    dq_far_ref,
    dt_ref,
    queries,
    mix,
    mix_turned,
):
    step = pl.program_id(0)
    count = near_ref.shape[1]
    rows = near_ref.shape[2]
    images, tile = e_ref.shape

    @pl.when(step == 0)
    def _():
        for q in range(count):
            queries[q * images : (q + 1) * images] = gather_members(near_ref, far_ref, q)
        dq_near_ref[...] = jnp.zeros_like(dq_near_ref)
        dq_far_ref[...] = jnp.zeros_like(dq_far_ref)

    half = 0.5 * (1.0 / heat_ref[0])
    e = e_ref[...]
    image = lax.broadcasted_iota(jnp.int32, (images, tile), 0)
    text = lax.broadcasted_iota(jnp.int32, (images, tile), 1) + step * tile - first_ref[0]
    target = jnp.where((image == text) & (image < rows), 0.9, 0.0) + 0.1 / total
    g = (e / row_ref[...] - target) * half + (e / column_ref[...] - target) * half
    slots = slot_ref[...].astype(jnp.float32)
    g_turned = g.T
    slots_turned = slots.T
    for q in range(count):
        mix[q * images : (q + 1) * images] = jnp.where(slots == float(q), g, 0.0).astype(jnp.bfloat16)
        mix_turned[:, q * images : (q + 1) * images] = jnp.where(
            slots_turned == float(q), g_turned, 0.0
        ).astype(jnp.bfloat16)
    dt_ref[...] = jnp.dot(mix_turned[...], queries[...], preferred_element_type=jnp.float32)
    texts = text_ref[...]
    group = 8
    for first in range(0, count, group):
        part = jnp.dot(
            mix[first * images : (first + group) * images], texts, preferred_element_type=jnp.float32
        )
        for k in range(group):
            for member in range(4):
                out = dq_near_ref if member < 2 else dq_far_ref
                start = k * images + member * rows
                out[member % 2, first + k] += part[start : start + rows]


def scores(heat, near, far, texts, slots):
    _, count, rows, width = near.shape
    images, held = slots.shape
    tile = min(256, held)
    whole = pl.BlockSpec((2, count, rows, width), lambda s: (0, 0, 0, 0))
    return pl.pallas_call(
        score_kernel,
        grid=(held // tile,),
        in_specs=[
            pl.BlockSpec(memory_space=pltpu.SMEM),
            whole,
            whole,
            pl.BlockSpec((tile, width), lambda s: (s, 0)),
            pl.BlockSpec((images, tile), lambda s: (0, s)),
        ],
        out_specs=[
            pl.BlockSpec((images, tile), lambda s: (0, s)),
            pl.BlockSpec((images, 1), lambda s: (0, 0)),
            pl.BlockSpec((1, tile), lambda s: (0, s)),
        ],
        out_shape=[
            jax.ShapeDtypeStruct((images, held), jnp.float32),
            jax.ShapeDtypeStruct((images, 1), jnp.float32),
            jax.ShapeDtypeStruct((1, held), jnp.float32),
        ],
        compiler_params=pltpu.CompilerParams(
            dimension_semantics=("arbitrary",), vmem_limit_bytes=VMEM_LIMIT
        ),
        name="scores",
    )(heat, near, far, texts, slots)


def gradients(total, heat, first, near, far, texts, slots, e, row, column):
    _, count, rows, width = near.shape
    images, held = slots.shape
    tile = min(512, held)
    whole = pl.BlockSpec((2, count, rows, width), lambda s: (0, 0, 0, 0))

    def body(*refs):
        grad_kernel(total, *refs)

    return pl.pallas_call(
        body,
        grid=(held // tile,),
        in_specs=[
            pl.BlockSpec(memory_space=pltpu.SMEM),
            pl.BlockSpec(memory_space=pltpu.SMEM),
            whole,
            whole,
            pl.BlockSpec((tile, width), lambda s: (s, 0)),
            pl.BlockSpec((images, tile), lambda s: (0, s)),
            pl.BlockSpec((images, tile), lambda s: (0, s)),
            pl.BlockSpec((images, 1), lambda s: (0, 0)),
            pl.BlockSpec((1, tile), lambda s: (0, s)),
        ],
        out_specs=[whole, whole, pl.BlockSpec((tile, width), lambda s: (s, 0))],
        out_shape=[
            jax.ShapeDtypeStruct(near.shape, jnp.float32),
            jax.ShapeDtypeStruct(near.shape, jnp.float32),
            jax.ShapeDtypeStruct((held, width), jnp.float32),
        ],
        scratch_shapes=[
            pltpu.VMEM((count * images, width), jnp.bfloat16),
            pltpu.VMEM((count * images, tile), jnp.bfloat16),
            pltpu.VMEM((tile, count * images), jnp.bfloat16),
        ],
        compiler_params=pltpu.CompilerParams(
            dimension_semantics=("arbitrary",), vmem_limit_bytes=VMEM_LIMIT
        ),
        name="gradients",
    )(heat, first, near, far, texts, slots, e, row, column)


def shards(picture_probes, caption_vectors, chosen_slot_per_match, softmax_heat):
    rows, count, width = picture_probes.shape
    total = chosen_slot_per_match.shape[1]
    fours = total // (4 * rows)
    held = fours * rows
    z_bit = lax.axis_index("zp")
    c_bit = lax.axis_index("c")

    q_unit, q_scale = normalized_rows(picture_probes)
    t_unit, t_scale = normalized_rows(caption_vectors)
    t_half = t_unit.astype(jnp.bfloat16)
    q_half = q_unit.astype(jnp.bfloat16).transpose(1, 0, 2)

    parts = chosen_slot_per_match.astype(jnp.bfloat16).reshape(rows, fours, 2, 2, rows)
    parts = parts.transpose(2, 3, 0, 1, 4).reshape(2, 2, rows, held)

    def part(z_flip, c_flip):
        by_z = jnp.where(z_bit == z_flip, parts[0], parts[1])
        return jnp.where(c_bit == c_flip, by_z[0], by_z[1])

    def swap_z(values):
        return lax.ppermute(values, "zp", SWAP)

    def swap_c(values):
        return lax.ppermute(values, "c", SWAP)

    q_other = swap_z(q_half)
    slots_other = swap_z(jnp.stack([part(1, 0), part(1, 1)]))
    texts = spread(spread(t_half, "zo"), "dp").reshape(held, width)
    near = jnp.stack([q_half, q_other])
    far = swap_c(near)
    slots_far = swap_c(jnp.stack([part(0, 1), slots_other[1]]))
    slots = jnp.concatenate([part(0, 0), slots_other[0], slots_far[0], slots_far[1]], axis=0)

    e, row, column = scores(softmax_heat, near, far, texts, slots)

    row = row.reshape(2, 2, rows)
    row = row + swap_c(row[::-1])
    row = row + swap_z(row[:, ::-1])
    column = jnp.sum(spread(column, "dp"), axis=0)
    column = jnp.sum(spread(column, "zo"), axis=0)

    place = lax.axis_index("dp") * lax.axis_size("zo") + lax.axis_index("zo")
    first = (place * rows).astype(jnp.int32).reshape(1)
    dq_near, dq_far, dt = gradients(
        total, softmax_heat, first, near, far, texts, slots, e, row.reshape(4 * rows, 1), column
    )

    dq_near = dq_near + swap_c(dq_far)
    dq_other = swap_z(dq_near[1])
    dt = dt.reshape(lax.axis_size("dp"), held // lax.axis_size("dp"), width)
    dt = jnp.sum(lax.all_to_all(dt, "dp", 0, 0, tiled=True), axis=0)
    dt = dt.reshape(lax.axis_size("zo"), rows, width)
    dt = jnp.sum(lax.all_to_all(dt, "zo", 0, 0, tiled=True), axis=0)
    text_grads = (dt - t_unit * jnp.sum(t_unit * dt, axis=-1, keepdims=True)) * t_scale
    dq = (dq_near[0] + dq_other).transpose(1, 0, 2)
    query_grads = (dq - q_unit * jnp.sum(q_unit * dq, axis=-1, keepdims=True)) * q_scale
    return (query_grads, text_grads)


def solution(mesh):
    groups, replicas = mesh.devices.shape
    axes = ("dp", "zo", "zp", "c")
    split = Mesh(mesh.devices.reshape(groups, replicas // 4, 2, 2), axes)
    return jax.shard_map(
        shards,
        mesh=split,
        in_specs=(P(axes, None, None), P(axes, None), P(axes, None), P()),
        out_specs=(P(axes, None, None), P(axes, None)),
        check_vma=False,
    )
```

```python
import jax
import jax.numpy as jnp
from jax import lax
from jax.experimental import pallas as pl
from jax.experimental.pallas import tpu as pltpu
from jax.sharding import Mesh
from jax.sharding import PartitionSpec as P

EPS = 1e-06
LANES = 128
VMEM_LIMIT = 56 * 1024 * 1024
SWAP = [(0, 1), (1, 0)]
PARAMS = pltpu.CompilerParams(dimension_semantics=("arbitrary",), vmem_limit_bytes=VMEM_LIMIT)
SMEM = pl.BlockSpec(memory_space=pltpu.SMEM)


def normalized_rows(values):
    wide = values.astype(jnp.float32)
    scale = lax.rsqrt(jnp.sum(wide * wide, axis=-1, keepdims=True) + EPS)
    return (wide * scale, scale)


def spread(values, axis):
    count = lax.axis_size(axis)
    return lax.all_to_all(jnp.broadcast_to(values[None], (count, *values.shape)), axis, 0, 0, tiled=True)


def whole_of(shape):
    return pl.BlockSpec(shape, lambda s: (0,) * len(shape))


def text_kernel(caption_ref, copies_ref):
    unit, _ = normalized_rows(caption_ref[...])
    half = unit.astype(jnp.bfloat16)
    for k in range(copies_ref.shape[0]):
        copies_ref[k] = half


def half_texts(captions, copies):
    return pl.pallas_call(
        text_kernel,
        out_shape=jax.ShapeDtypeStruct((copies, *captions.shape), jnp.bfloat16),
        name="half_texts",
    )(captions)


def query_kernel(probe_ref, half_ref, units):
    rows, count, width = probe_ref.shape
    unit, _ = normalized_rows(probe_ref[...])
    unit = unit.reshape(rows * count, width)
    for k in range(width // LANES):
        at = slice(k * LANES, (k + 1) * LANES)
        units[k] = unit[:, at]
        for q in range(count):
            half_ref[q, :, at] = units[k, pl.ds(q, rows, stride=count), :].astype(jnp.bfloat16)


def half_queries(probes):
    rows, count, width = probes.shape
    block = min(16, rows)
    return pl.pallas_call(
        query_kernel,
        grid=(rows // block,),
        in_specs=[pl.BlockSpec((block, count, width), lambda s: (s, 0, 0))],
        out_specs=pl.BlockSpec((count, block, width), lambda s: (0, s, 0)),
        out_shape=jax.ShapeDtypeStruct((count, rows, width), jnp.bfloat16),
        scratch_shapes=[pltpu.VMEM((width // LANES, block * count, LANES), jnp.float32)],
        compiler_params=PARAMS,
        name="half_queries",
    )(probes)


def slot_kernel(bits_ref, slot_ref, own_ref, core_ref, chip_ref, order):
    rows, wide = slot_ref.shape
    lanes = 4 * rows
    block = 4 * lanes

    @pl.when(pl.program_id(0) == 0)
    def _():
        source = lax.broadcasted_iota(jnp.int32, (block, block), 0)
        goal = lax.broadcasted_iota(jnp.int32, (block, block), 1)
        member = (goal // lanes) ^ bits_ref[0]
        wanted = (goal % lanes) // rows * lanes + member * rows + goal % rows
        order[...] = jnp.where(source == wanted, 1.0, 0.0).astype(jnp.bfloat16)

    for k in range(wide // block):
        piece = slot_ref[:, k * block : (k + 1) * block].astype(jnp.float32).astype(jnp.bfloat16)
        moved = jnp.dot(piece, order[...], preferred_element_type=jnp.float32).astype(jnp.bfloat16)
        at = slice(k * lanes, (k + 1) * lanes)
        own_ref[:, at] = moved[:, :lanes]
        core_ref[:, at] = moved[:, lanes : 2 * lanes]
        chip_ref[0, :, at] = moved[:, 2 * lanes : 3 * lanes]
        chip_ref[1, :, at] = moved[:, 3 * lanes :]


def slot_parts(bits, slots):
    rows, total = slots.shape
    held = total // 4
    steps = max(1, total // (64 * rows))
    out = jax.ShapeDtypeStruct((rows, held), jnp.bfloat16)
    pair = jax.ShapeDtypeStruct((2, rows, held), jnp.bfloat16)
    spec = pl.BlockSpec((rows, held // steps), lambda s: (0, s))
    return pl.pallas_call(
        slot_kernel,
        grid=(steps,),
        in_specs=[SMEM, pl.BlockSpec((rows, total // steps), lambda s: (0, s))],
        out_specs=[spec, spec, pl.BlockSpec((2, rows, held // steps), lambda s: (0, 0, s))],
        out_shape=[out, out, pair],
        scratch_shapes=[pltpu.VMEM((16 * rows, 16 * rows), jnp.bfloat16)],
        compiler_params=PARAMS,
        name="slot_parts",
    )(bits, slots)


def slots_of(refs):
    return jnp.concatenate([ref[...].reshape(ref.shape[-2:]) for ref in refs], axis=0).astype(jnp.float32)


def score_kernel(heat_ref, *refs):
    query_refs, slot_refs, (text_ref, e_ref, row_ref, column_ref) = refs[:4], refs[4:8], refs[8:]
    count = query_refs[0].shape[0]
    images = e_ref.shape[0]
    group = 4
    slots = slots_of(slot_refs)
    texts = text_ref[...]
    picked = jnp.zeros(e_ref.shape, jnp.float32)
    for first in range(0, count, group):
        queries = jnp.concatenate(
            [ref[first + k] for k in range(group) for ref in query_refs], axis=0
        )
        dense = lax.dot_general(
            queries, texts, (((1,), (1,)), ((), ())), preferred_element_type=jnp.float32
        )
        for k in range(group):
            picked = jnp.where(slots == float(first + k), dense[k * images : (k + 1) * images], picked)
    e = jnp.exp(picked * (1.0 / heat_ref[0]))
    e_ref[...] = e
    column_ref[...] = jnp.sum(e, axis=0, keepdims=True)

    @pl.when(pl.program_id(0) == 0)
    def _():
        row_ref[...] = jnp.zeros_like(row_ref)

    row_ref[...] += jnp.sum(e, axis=1, keepdims=True)


def slot_specs(rows, tile):
    return [
        pl.BlockSpec((rows, tile), lambda s: (0, s)),
        pl.BlockSpec((1, rows, tile), lambda s: (0, 0, s)),
        pl.BlockSpec((rows, tile), lambda s: (0, s)),
        pl.BlockSpec((1, rows, tile), lambda s: (1, 0, s)),
    ]


def scores(heat, queries, slots, texts):
    count, rows, width = queries[0].shape
    held = texts.shape[0]
    images = 4 * rows
    tile = min(256, held)
    return pl.pallas_call(
        score_kernel,
        grid=(held // tile,),
        in_specs=[SMEM]
        + [whole_of((count, rows, width))] * 4
        + slot_specs(rows, tile)
        + [pl.BlockSpec((tile, width), lambda s: (s, 0))],
        out_specs=[
            pl.BlockSpec((images, tile), lambda s: (0, s)),
            pl.BlockSpec((images, 1), lambda s: (0, 0)),
            pl.BlockSpec((1, tile), lambda s: (0, s)),
        ],
        out_shape=[
            jax.ShapeDtypeStruct((images, held), jnp.float32),
            jax.ShapeDtypeStruct((images, 1), jnp.float32),
            jax.ShapeDtypeStruct((1, held), jnp.float32),
        ],
        compiler_params=PARAMS,
        name="scores",
    )(heat, *queries, *slots, texts)


def score_gradient(total, rows, heat_ref, first_ref, e_ref, row_ref, column_ref):
    images, tile = e_ref.shape
    half = 0.5 * (1.0 / heat_ref[0])
    e = e_ref[...]
    image = lax.broadcasted_iota(jnp.int32, (images, tile), 0)
    text = lax.broadcasted_iota(jnp.int32, (images, tile), 1) + pl.program_id(0) * tile - first_ref[0]
    target = jnp.where((image == text) & (image < rows), 0.9, 0.0) + 0.1 / total
    return (e / row_ref[...] - target) * half + (e / column_ref[...] - target) * half


def text_grad_kernel(total, heat_ref, first_ref, *refs):
    query_refs, slot_refs, (e_ref, row_ref, column_ref, dt_ref, queries, mix) = refs[:4], refs[4:8], refs[8:]
    count, rows, _ = query_refs[0].shape
    images = 4 * rows

    @pl.when(pl.program_id(0) == 0)
    def _():
        for q in range(count):
            for member, ref in enumerate(query_refs):
                start = q * images + member * rows
                queries[start : start + rows] = ref[q]

    g = score_gradient(total, rows, heat_ref, first_ref, e_ref, row_ref, column_ref).T
    slots = slots_of(slot_refs).T
    for q in range(count):
        mix[:, q * images : (q + 1) * images] = jnp.where(slots == float(q), g, 0.0).astype(jnp.bfloat16)
    dt_ref[...] = jnp.dot(mix[...], queries[...], preferred_element_type=jnp.float32)


def query_grad_kernel(total, heat_ref, first_ref, *refs):
    slot_refs, (text_ref, e_ref, row_ref, column_ref), outs, mix = refs[:4], refs[4:8], refs[8:11], refs[11]
    rows = slot_refs[0].shape[-2]
    images = 4 * rows
    count = outs[0].shape[0]
    g = score_gradient(total, rows, heat_ref, first_ref, e_ref, row_ref, column_ref)
    slots = slots_of(slot_refs)

    @pl.when(pl.program_id(0) == 0)
    def _():
        for out in outs:
            out[...] = jnp.zeros_like(out)

    for q in range(count):
        mix[q * images : (q + 1) * images] = jnp.where(slots == float(q), g, 0.0).astype(jnp.bfloat16)
    texts = text_ref[...]
    group = 8
    for first in range(0, count, group):
        part = jnp.dot(
            mix[first * images : (first + group) * images], texts, preferred_element_type=jnp.float32
        )
        for k in range(group):
            at = k * images
            outs[0][first + k] += part[at : at + rows]
            outs[1][first + k] += part[at + rows : at + 2 * rows]
            outs[2][0, first + k] += part[at + 2 * rows : at + 3 * rows]
            outs[2][1, first + k] += part[at + 3 * rows : at + 4 * rows]


def text_gradients(total, heat, first, queries, slots, e, row, column):
    count, rows, width = queries[0].shape
    images, held = e.shape
    tile = min(512, held)

    def body(*refs):
        text_grad_kernel(total, *refs)

    return pl.pallas_call(
        body,
        grid=(held // tile,),
        in_specs=[SMEM, SMEM]
        + [whole_of((count, rows, width))] * 4
        + slot_specs(rows, tile)
        + [
            pl.BlockSpec((images, tile), lambda s: (0, s)),
            whole_of((images, 1)),
            pl.BlockSpec((1, tile), lambda s: (0, s)),
        ],
        out_specs=pl.BlockSpec((tile, width), lambda s: (s, 0)),
        out_shape=jax.ShapeDtypeStruct((held, width), jnp.float32),
        scratch_shapes=[
            pltpu.VMEM((count * images, width), jnp.bfloat16),
            pltpu.VMEM((tile, count * images), jnp.bfloat16),
        ],
        compiler_params=PARAMS,
        name="text_gradients",
    )(heat, first, *queries, *slots, e, row, column)


def query_gradients(total, count, heat, first, slots, texts, e, row, column):
    images, held = e.shape
    rows = images // 4
    width = texts.shape[1]
    tile = min(512, held)
    one = (count, rows, width)

    def body(*refs):
        query_grad_kernel(total, *refs)

    return pl.pallas_call(
        body,
        grid=(held // tile,),
        in_specs=[SMEM, SMEM]
        + slot_specs(rows, tile)
        + [
            pl.BlockSpec((tile, width), lambda s: (s, 0)),
            pl.BlockSpec((images, tile), lambda s: (0, s)),
            whole_of((images, 1)),
            pl.BlockSpec((1, tile), lambda s: (0, s)),
        ],
        out_specs=[whole_of(one), whole_of(one), whole_of((2, *one))],
        out_shape=[
            jax.ShapeDtypeStruct(one, jnp.float32),
            jax.ShapeDtypeStruct(one, jnp.float32),
            jax.ShapeDtypeStruct((2, *one), jnp.float32),
        ],
        scratch_shapes=[pltpu.VMEM((count * images, tile), jnp.bfloat16)],
        compiler_params=PARAMS,
        name="query_gradients",
    )(heat, first, *slots, texts, e, row, column)


def finish_kernel(probe_ref, own_ref, core_ref, chip_ref, out_ref, total):
    block, count, width = probe_ref.shape
    added = (own_ref[...] + core_ref[0] + chip_ref[...]).reshape(count * block, width)
    halves = range(width // LANES)
    for k in halves:
        total[k] = added[:, k * LANES : (k + 1) * LANES]
    for i in range(block):
        unit, scale = normalized_rows(probe_ref[i])
        dq = jnp.concatenate([total[k, pl.ds(i, count, stride=block), :] for k in halves], axis=1)
        out_ref[i] = (dq - unit * jnp.sum(unit * dq, axis=-1, keepdims=True)) * scale


def finish_queries(probes, own, core, chip):
    rows, count, width = probes.shape
    block = min(8, rows)
    moved = pl.BlockSpec((count, block, width), lambda s: (0, s, 0))
    kept = pl.BlockSpec((block, count, width), lambda s: (s, 0, 0))
    return pl.pallas_call(
        finish_kernel,
        grid=(rows // block,),
        in_specs=[kept, moved, pl.BlockSpec((1, count, block, width), lambda s: (0, 0, s, 0)), moved],
        out_specs=kept,
        out_shape=jax.ShapeDtypeStruct(probes.shape, jnp.float32),
        scratch_shapes=[pltpu.VMEM((width // LANES, count * block, LANES), jnp.float32)],
        compiler_params=PARAMS,
        name="finish_queries",
    )(probes, own, core, chip)


def swap_z(values):
    return lax.ppermute(values, "zp", SWAP)


def swap_c(values):
    return lax.ppermute(values, "c", SWAP)


def shards(picture_probes, caption_vectors, chosen_slot_per_match, softmax_heat):
    rows, count, width = picture_probes.shape
    total = chosen_slot_per_match.shape[1]
    held = total // 4
    groups, outer = lax.axis_size("dp"), lax.axis_size("zo")

    text_copies = half_texts(caption_vectors, outer)
    texts = lax.all_to_all(text_copies, "zo", 0, 0, tiled=True)
    texts = spread(texts.reshape(outer * rows, width), "dp").reshape(held, width)

    bits = (lax.axis_index("zp") * 2 + lax.axis_index("c")).astype(jnp.int32).reshape(1)
    q_own = half_queries(picture_probes)
    slots_own, slots_core, slots_chip = slot_parts(bits, chosen_slot_per_match)
    q_chip = swap_z(q_own)
    slots_chip = swap_z(slots_chip)
    queries = (q_own, q_chip, swap_c(q_own), swap_c(q_chip))
    slots = (slots_own, slots_chip, swap_c(slots_core), swap_c(slots_chip))

    e, row, column = scores(softmax_heat, queries, slots, texts)

    row = row.reshape(2, 2, rows)
    row = row + swap_c(row[::-1])
    row = row + swap_z(row[:, ::-1])
    row = row.reshape(4 * rows, 1)
    column = jnp.sum(spread(column, "dp"), axis=0)
    column = jnp.sum(spread(column, "zo"), axis=0)

    place = lax.axis_index("dp") * outer + lax.axis_index("zo")
    first = (place * rows).astype(jnp.int32).reshape(1)
    dt = text_gradients(total, softmax_heat, first, queries, slots, e, row, column)
    dt = lax.all_to_all(dt.reshape(groups, outer * rows, width), "dp", 0, 0, tiled=True)
    dq_own, dq_chip, dq_far = query_gradients(
        total, count, softmax_heat, first, slots, texts, e, row, column
    )
    dq_near = swap_c(dq_far)
    dq_chip = swap_z(dq_chip + dq_near[1])
    dt = jnp.sum(dt, axis=0).reshape(outer, rows, width)
    dt = lax.all_to_all(dt, "zo", 0, 0, tiled=True)
    query_grads = finish_queries(picture_probes, dq_own, dq_near, dq_chip)
    dt, query_grads = lax.optimization_barrier((dt, query_grads))
    dt = jnp.sum(dt, axis=0)
    t_unit, t_scale = normalized_rows(caption_vectors)
    text_grads = (dt - t_unit * jnp.sum(t_unit * dt, axis=-1, keepdims=True)) * t_scale
    return (query_grads, text_grads)


def solution(mesh):
    groups, replicas = mesh.devices.shape
    axes = ("dp", "zo", "zp", "c")
    split = Mesh(mesh.devices.reshape(groups, replicas // 4, 2, 2), axes)
    return jax.shard_map(
        shards,
        mesh=split,
        in_specs=(P(axes, None, None), P(axes, None), P(axes, None), P()),
        out_specs=(P(axes, None, None), P(axes, None)),
        check_vma=False,
    )
```

```python
import jax
import jax.numpy as jnp
from jax import lax
from jax.experimental import pallas as pl
from jax.experimental.pallas import tpu as pltpu
from jax.sharding import Mesh
from jax.sharding import PartitionSpec as P

EPS = 1e-06
LANES = 128
HALF = jnp.float16
SENT = 16.0
SWAP = [(0, 1), (1, 0)]
SMEM = pl.BlockSpec(memory_space=pltpu.SMEM)
VMEM = pl.BlockSpec(memory_space=pltpu.VMEM)


def params(mib):
    return pltpu.CompilerParams(vmem_limit_bytes=mib * 1024 * 1024)


def normalized_rows(values):
    wide = values.astype(jnp.float32)
    scale = lax.rsqrt(jnp.sum(wide * wide, axis=-1, keepdims=True) + EPS)
    return (wide * scale, scale)


def text_kernel(caption_ref, copies_ref):
    unit, _ = normalized_rows(caption_ref[...])
    half = unit.astype(jnp.bfloat16)
    for k in range(copies_ref.shape[0]):
        copies_ref[k] = half


def half_texts(captions, copies):
    return pl.pallas_call(
        text_kernel,
        in_specs=[VMEM],
        out_specs=VMEM,
        out_shape=jax.ShapeDtypeStruct((copies, *captions.shape), jnp.bfloat16),
        compiler_params=params(16),
        name="half_texts",
    )(captions)


def query_kernel(probe_ref, half_ref, units):
    rows, count, width = probe_ref.shape
    unit, _ = normalized_rows(probe_ref[...])
    unit = unit.reshape(rows * count, width)
    here = pl.ds(pl.multiple_of(pl.program_id(0) * rows, rows), rows)
    for k in range(width // LANES):
        at = slice(k * LANES, (k + 1) * LANES)
        units[k] = unit[:, at]
        for q in range(count):
            half_ref[q, here, at] = units[k, pl.ds(q, rows, stride=count), :].astype(jnp.bfloat16)


def half_queries(probes):
    rows, count, width = probes.shape
    block = min(16, rows)
    return pl.pallas_call(
        query_kernel,
        grid=(rows // block,),
        in_specs=[pl.BlockSpec((block, count, width), lambda s: (s, 0, 0))],
        out_specs=VMEM,
        out_shape=jax.ShapeDtypeStruct((count, rows, width), jnp.bfloat16),
        scratch_shapes=[pltpu.VMEM((width // LANES, block * count, LANES), jnp.float32)],
        compiler_params=params(16),
        name="half_queries",
    )(probes)


def slot_kernel(bits_ref, slot_ref, own_ref, core_ref, chip_ref, order):
    rows, wide = slot_ref.shape
    lanes = 4 * rows
    block = 4 * lanes

    @pl.when(pl.program_id(0) == 0)
    def _():
        source = lax.broadcasted_iota(jnp.int32, (block, block), 0)
        goal = lax.broadcasted_iota(jnp.int32, (1, block), 1)
        member = (goal // lanes) ^ bits_ref[0]
        wanted = (goal % lanes) // rows * lanes + member * rows + goal % rows
        order[...] = jnp.where(source == wanted, 1.0, 0.0).astype(jnp.bfloat16)

    blocks = wide // block
    pieces = [slot_ref[:, k * block : (k + 1) * block] for k in range(blocks)]
    pieces = jnp.concatenate(pieces, axis=0).astype(jnp.float32).astype(jnp.bfloat16)
    moved = jnp.dot(pieces, order[...], preferred_element_type=jnp.float32).astype(jnp.bfloat16)
    for k in range(blocks):
        at = pl.ds(pl.multiple_of((pl.program_id(0) * blocks + k) * lanes, lanes), lanes)
        piece = moved[k * rows : (k + 1) * rows]
        own_ref[:, at] = piece[:, :lanes]
        core_ref[:, at] = piece[:, lanes : 2 * lanes]
        chip_ref[0, :, at] = piece[:, 2 * lanes : 3 * lanes]
        chip_ref[1, :, at] = piece[:, 3 * lanes :]


def slot_parts(bits, slots):
    rows, total = slots.shape
    held = total // 4
    steps = 4 if total >= 64 * rows else 1
    out = jax.ShapeDtypeStruct((rows, held), jnp.bfloat16)
    pair = jax.ShapeDtypeStruct((2, rows, held), jnp.bfloat16)
    return pl.pallas_call(
        slot_kernel,
        grid=(steps,),
        in_specs=[SMEM, pl.BlockSpec((rows, total // steps), lambda s: (0, s))],
        out_specs=[VMEM, VMEM, VMEM],
        out_shape=[out, out, pair],
        scratch_shapes=[pltpu.VMEM((16 * rows, 16 * rows), jnp.bfloat16)],
        compiler_params=params(16),
        name="slot_parts",
    )(bits, slots)


def slots_at(refs, at):
    own, core, chip, both = refs
    return jnp.concatenate([own[:, at], core[:, at], chip[0, :, at], both[1, :, at]], axis=0).astype(jnp.float32)


def score_kernel(tile, group, heat_ref, *refs):
    query_refs, slot_refs = refs[:4], refs[4:8]
    text_ref, stack_ref, e_ref, row_ref, column_ref = refs[8:]
    count, rows, _ = query_refs[0].shape
    images, held = e_ref.shape
    row_ref[...] = jnp.zeros_like(row_ref)
    for q in range(count):
        for member, ref in enumerate(query_refs):
            start = q * images + member * rows
            stack_ref[start : start + rows] = ref[q]

    @pl.loop(0, held // tile)
    def _(step):
        at = pl.ds(pl.multiple_of(step * tile, tile), tile)
        slots = slots_at(slot_refs, at)
        texts = text_ref[at, :]
        picked = jnp.zeros((images, tile), jnp.float32)
        for first in range(0, count, group):
            queries = stack_ref[first * images : (first + group) * images]
            dense = lax.dot_general(
                queries, texts, (((1,), (1,)), ((), ())), preferred_element_type=jnp.float32
            )
            for k in range(group):
                part = dense[k * images : (k + 1) * images]
                picked = jnp.where(slots == float(first + k), part, picked)
        e = jnp.exp(picked * (1.0 / heat_ref[0]))
        e_ref[:, at] = e
        total = jnp.sum(e, axis=0, keepdims=True)
        for k in range(column_ref.shape[0]):
            column_ref[k, :, at] = total
        row_ref[...] += jnp.sum(e, axis=1, keepdims=True)


def scores(copies, heat, queries, slots, texts):
    count, rows, width = queries[0].shape
    held = texts.shape[0]
    images = 4 * rows
    tile = min(512, held)

    def body(*refs):
        score_kernel(tile, 4, *refs)

    return pl.pallas_call(
        body,
        in_specs=[SMEM] + [VMEM] * 9,
        out_specs=[VMEM] * 4,
        out_shape=[
            jax.ShapeDtypeStruct((count * images, width), jnp.bfloat16),
            jax.ShapeDtypeStruct((images, held), jnp.float32),
            jax.ShapeDtypeStruct((images, 1), jnp.float32),
            jax.ShapeDtypeStruct((copies, 1, held), jnp.float32),
        ],
        compiler_params=params(24),
        name="scores",
    )(heat, *queries, *slots, texts)


def column_kernel(column_ref, copies_ref):
    total = jnp.sum(column_ref[...], axis=0, keepdims=True)
    for k in range(copies_ref.shape[0]):
        copies_ref[k] = total


def column_sums(columns, copies):
    held = columns.shape[-1]
    return pl.pallas_call(
        column_kernel,
        in_specs=[VMEM],
        out_specs=VMEM,
        out_shape=jax.ShapeDtypeStruct((copies, 1, held), jnp.float32),
        compiler_params=params(16),
        name="column_sums",
    )(columns.reshape(-1, held))


def row_totals(row_refs):
    rows = row_refs[0].shape[0] // 4
    members = []
    for member in range(4):
        parts = [ref[(member ^ k) * rows : ((member ^ k) + 1) * rows] for k, ref in enumerate(row_refs)]
        members.append((parts[0] + parts[1]) + (parts[2] + parts[3]))
    return jnp.concatenate(members, axis=0)


def score_gradient(total, heat_ref, e, row, columns, target):
    half = 0.5 * (1.0 / heat_ref[0])
    column = jnp.sum(columns, axis=0)
    return (e / row - target) * half + (e / column - target) * half


def smooth_target(total, rows, shape, start):
    image = lax.broadcasted_iota(jnp.int32, shape, 0)
    text = lax.broadcasted_iota(jnp.int32, shape, 1) + start
    return jnp.where((image == text) & (image < rows), 0.9, 0.0) + 0.1 / total


def text_grad_kernel(total, heat_ref, first_ref, stack_ref, *refs):
    slot_refs, row_refs, (e_ref, column_ref, dt_ref, mark_ref, mix) = refs[:4], refs[4:8], refs[8:]
    images = e_ref.shape[0]
    tile, depth = mix.shape
    start = pl.multiple_of(pl.program_id(0) * tile, tile)
    at = pl.ds(start, tile)
    target = smooth_target(total, images // 4, (images, tile), start - first_ref[0])
    g = score_gradient(total, heat_ref, e_ref[:, at], row_totals(row_refs), column_ref[:, :, at], target).T
    slots = slots_at(slot_refs, at).T
    for q in range(depth // images):
        mix[:, q * images : (q + 1) * images] = jnp.where(slots == float(q), g, 0.0).astype(jnp.bfloat16)
    dt_ref[...] = jnp.dot(mix[...], stack_ref[...], preferred_element_type=jnp.float32) * SENT
    mark_ref[...] = dt_ref[:8, :LANES]


def text_gradients(total, heat, first, stack, slots, rows, e, column):
    depth, width = stack.shape
    held = e.shape[1]
    tile = min(512, held)

    def body(*refs):
        text_grad_kernel(total, *refs)

    return pl.pallas_call(
        body,
        grid=(held // tile,),
        in_specs=[SMEM, SMEM] + [VMEM] * 11,
        out_specs=[pl.BlockSpec((tile, width), lambda s: (s, 0)), VMEM],
        out_shape=[
            jax.ShapeDtypeStruct((held, width), jnp.float32),
            jax.ShapeDtypeStruct((8, LANES), jnp.float32),
        ],
        scratch_shapes=[pltpu.VMEM((tile, depth), jnp.bfloat16)],
        compiler_params=params(28),
        name="text_gradients",
    )(heat, first, stack, *slots, *rows, e, column)


def query_grad_kernel(total, low, heat_ref, mark_ref, *refs):
    slot_refs, row_refs, (text_ref, e_ref, column_ref), outs, mix = refs[:4], refs[4:8], refs[8:11], refs[11:-1], refs[-1]
    count, rows, _ = outs[0].shape
    images = len(outs) * rows
    group = mix.shape[0] // images
    at = slice(low * rows, low * rows + images)
    slots = slots_at(slot_refs, slice(None))[at]
    row = row_totals(row_refs)[at]
    g = score_gradient(total, heat_ref, e_ref[at], row, column_ref[...], 0.1 / total)
    texts = text_ref[...]
    for first in range(0, count, group):
        for k in range(group):
            kept = jnp.where(slots == float(first + k), g, 0.0)
            mix[k * images : (k + 1) * images] = kept.astype(jnp.bfloat16)
        part = jnp.dot(mix[...], texts, preferred_element_type=jnp.float32)
        for k in range(group):
            for member, out in enumerate(outs):
                at = k * images + member * rows
                out[first + k] = part[at : at + rows]


def query_gradients(total, count, low, members, heat, mark, slots, row_parts, texts, e, column):
    images, held = e.shape
    rows = images // 4
    width = texts.shape[1]
    group = 8

    def body(*refs):
        query_grad_kernel(total, low, *refs)

    return pl.pallas_call(
        body,
        in_specs=[SMEM, pl.BlockSpec(memory_space=pl.ANY)] + [VMEM] * 11,
        out_specs=[VMEM] * members,
        out_shape=[jax.ShapeDtypeStruct((count, rows, width), jnp.float32)] * members,
        scratch_shapes=[pltpu.VMEM((group * members * rows, held), jnp.bfloat16)],
        compiler_params=params(28),
        name="query_gradients",
    )(heat, mark, *slots, *row_parts, texts, e, column)


def finish_kernel(total, heat_ref, first_ref, probe_ref, slot_ref, *refs):
    row_refs, (text_ref, e_ref, column_ref, core_ref, chip_ref, out_ref, mix, sums) = refs[:4], refs[4:]
    block, count, width = probe_ref.shape
    held = e_ref.shape[1]
    start = pl.multiple_of(pl.program_id(0) * block, block)
    here = pl.ds(start, block)
    rows = slot_ref.shape[0]
    row = sum(ref[pl.ds(k * rows + start, block), :] for k, ref in enumerate(row_refs))
    image = lax.broadcasted_iota(jnp.int32, (block, held), 0) + start
    text = lax.broadcasted_iota(jnp.int32, (block, held), 1) - first_ref[0]
    target = jnp.where(image == text, 0.9, 0.0) + 0.1 / total
    g = score_gradient(total, heat_ref, e_ref[here, :], row, column_ref[...], target)
    slots = slot_ref[here, :].astype(jnp.float32)
    for q in range(count):
        mix[q * block : (q + 1) * block] = jnp.where(slots == float(q), g, 0.0).astype(jnp.bfloat16)
    added = jnp.dot(mix[...], text_ref[...], preferred_element_type=jnp.float32)
    added += (core_ref[:, here, :] + chip_ref[:, here, :].astype(jnp.float32)).reshape(count * block, width)
    halves = range(width // LANES)
    for k in halves:
        sums[k] = added[:, k * LANES : (k + 1) * LANES]
    for i in range(block):
        unit, scale = normalized_rows(probe_ref[i])
        dq = jnp.concatenate([sums[k, pl.ds(i, count, stride=block), :] for k in halves], axis=1)
        out_ref[i] = (dq - unit * jnp.sum(unit * dq, axis=-1, keepdims=True)) * scale


def finish_queries(total, heat, first, probes, slots, row_parts, texts, e, column, core, chip):
    rows, count, width = probes.shape
    block = min(16, rows)
    kept = pl.BlockSpec((block, count, width), lambda s: (s, 0, 0))

    def body(*refs):
        finish_kernel(total, *refs)

    return pl.pallas_call(
        body,
        grid=(rows // block,),
        in_specs=[SMEM, SMEM, kept] + [VMEM] * 10,
        out_specs=kept,
        out_shape=jax.ShapeDtypeStruct(probes.shape, jnp.float32),
        scratch_shapes=[
            pltpu.VMEM((count * block, e.shape[1]), jnp.bfloat16),
            pltpu.VMEM((width // LANES, count * block, LANES), jnp.float32),
        ],
        compiler_params=params(24),
        name="finish_queries",
    )(heat, first, probes, slots, *row_parts, texts, e, column, core, chip)


def finish_text_kernel(caption_ref, block_ref, out_ref):
    unit, scale = normalized_rows(caption_ref[...])
    dt = jnp.sum(block_ref[...], axis=0) * (1.0 / SENT)
    out_ref[...] = (dt - unit * jnp.sum(unit * dt, axis=-1, keepdims=True)) * scale


def finish_texts(captions, blocks):
    return pl.pallas_call(
        finish_text_kernel,
        in_specs=[VMEM, VMEM],
        out_specs=VMEM,
        out_shape=jax.ShapeDtypeStruct(captions.shape, jnp.float32),
        compiler_params=params(16),
        name="finish_texts",
    )(captions, blocks)


def swap_z(values):
    return lax.ppermute(values, "zp", SWAP)


def swap_c(values):
    return lax.ppermute(values, "c", SWAP)


def shards(picture_probes, caption_vectors, chosen_slot_per_match, softmax_heat):
    rows, count, width = picture_probes.shape
    total = chosen_slot_per_match.shape[1]
    held = total // 4
    groups, outer = lax.axis_size("dp"), lax.axis_size("zo")

    texts = lax.all_to_all(half_texts(caption_vectors, outer), "zo", 0, 0, tiled=True)
    texts = jnp.broadcast_to(texts.reshape(1, outer * rows, width), (groups, outer * rows, width))
    texts = lax.all_to_all(texts, "dp", 0, 0, tiled=True).reshape(held, width)

    bits = (lax.axis_index("zp") * 2 + lax.axis_index("c")).astype(jnp.int32).reshape(1)
    q_own = half_queries(picture_probes)
    slots_own, slots_core, slots_chip = slot_parts(bits, chosen_slot_per_match)
    q_chip = swap_z(q_own)
    slots_chip = swap_z(slots_chip)
    queries = (q_own, swap_c(q_own), q_chip, swap_c(q_chip))
    slots = (slots_own, swap_c(slots_core), slots_chip, swap_c(slots_chip))

    stack, e, row, column = scores(groups, softmax_heat, queries, slots, texts)

    row_chip = swap_z(row)
    row_parts = (row, swap_c(row), row_chip, swap_c(row_chip))
    column = lax.all_to_all(column, "dp", 0, 0, tiled=True)
    column = lax.all_to_all(column_sums(column, outer), "zo", 0, 0, tiled=True)

    place = lax.axis_index("dp") * outer + lax.axis_index("zo")
    first = (place * rows).astype(jnp.int32).reshape(1)
    dt, mark = text_gradients(total, softmax_heat, first, stack, slots, row_parts, e, column)
    dt = lax.all_to_all(dt.astype(HALF).reshape(groups, outer * rows, width), "dp", 0, 0, tiled=True)
    common = (row_parts, texts, e, column)
    dq_chip, dq_both = query_gradients(total, count, 2, 2, softmax_heat, first, slots, *common)
    dq_chip = swap_z((dq_chip + swap_c(dq_both)).astype(HALF)).astype(jnp.float32)
    (dq_core,) = query_gradients(total, count, 1, 1, softmax_heat, mark, slots, *common)
    dq_core = swap_c(dq_core)
    dt = jnp.sum(dt.astype(jnp.float32), axis=0).reshape(outer, rows, width)
    dt = lax.all_to_all(dt, "zo", 0, 0, tiled=True)
    query_grads = finish_queries(
        total, softmax_heat, first, picture_probes, slots[0], *common, dq_core, dq_chip
    )
    dt, query_grads = lax.optimization_barrier((dt, query_grads))
    text_grads = finish_texts(caption_vectors, dt)
    return (query_grads, text_grads)


def solution(mesh):
    groups, replicas = mesh.devices.shape
    axes = ("dp", "zo", "zp", "c")
    split = Mesh(mesh.devices.reshape(groups, replicas // 4, 2, 2), axes)
    return jax.shard_map(
        shards,
        mesh=split,
        in_specs=(P(axes, None, None), P(axes, None), P(axes, None), P()),
        out_specs=(P(axes, None, None), P(axes, None)),
        check_vma=False,
    )
```

```python
import jax
import jax.numpy as jnp
from jax import lax
from jax.experimental import pallas as pl
from jax.experimental.pallas import tpu as pltpu
from jax.sharding import Mesh
from jax.sharding import PartitionSpec as P

EPS = 1e-06
LANES = 128
HALF = jnp.float16
SENT = 16.0
SWAP = [(0, 1), (1, 0)]
SMEM = pl.BlockSpec(memory_space=pltpu.SMEM)
VMEM = pl.BlockSpec(memory_space=pltpu.VMEM)


def params(mib):
    return pltpu.CompilerParams(vmem_limit_bytes=mib * 1024 * 1024)


def normalized_rows(values):
    wide = values.astype(jnp.float32)
    scale = lax.rsqrt(jnp.sum(wide * wide, axis=-1, keepdims=True) + EPS)
    return (wide * scale, scale)


def text_kernel(caption_ref, copies_ref):
    unit, _ = normalized_rows(caption_ref[...])
    half = unit.astype(jnp.bfloat16)
    for k in range(copies_ref.shape[0]):
        copies_ref[k] = half


def half_texts(captions, copies):
    return pl.pallas_call(
        text_kernel,
        in_specs=[VMEM],
        out_specs=VMEM,
        out_shape=jax.ShapeDtypeStruct((copies, *captions.shape), jnp.bfloat16),
        compiler_params=params(16),
        name="half_texts",
    )(captions)


def query_kernel(probe_ref, half_ref, units):
    rows, count, width = probe_ref.shape
    unit, _ = normalized_rows(probe_ref[...])
    unit = unit.reshape(rows * count, width)
    here = pl.ds(pl.multiple_of(pl.program_id(0) * rows, rows), rows)
    for k in range(width // LANES):
        at = slice(k * LANES, (k + 1) * LANES)
        units[k] = unit[:, at]
        for q in range(count):
            half_ref[q, here, at] = units[k, pl.ds(q, rows, stride=count), :].astype(jnp.bfloat16)


def half_queries(probes):
    rows, count, width = probes.shape
    block = min(16, rows)
    return pl.pallas_call(
        query_kernel,
        grid=(rows // block,),
        in_specs=[pl.BlockSpec((block, count, width), lambda s: (s, 0, 0))],
        out_specs=VMEM,
        out_shape=jax.ShapeDtypeStruct((count, rows, width), jnp.bfloat16),
        scratch_shapes=[pltpu.VMEM((width // LANES, block * count, LANES), jnp.float32)],
        compiler_params=params(16),
        name="half_queries",
    )(probes)


def slot_kernel(bits_ref, slot_ref, own_ref, core_ref, chip_ref, order):
    rows, wide = slot_ref.shape
    lanes = 4 * rows
    block = 4 * lanes

    @pl.when(pl.program_id(0) == 0)
    def _():
        source = lax.broadcasted_iota(jnp.int32, (block, block), 0)
        goal = lax.broadcasted_iota(jnp.int32, (1, block), 1)
        member = (goal // lanes) ^ bits_ref[0]
        wanted = (goal % lanes) // rows * lanes + member * rows + goal % rows
        order[...] = jnp.where(source == wanted, 1.0, 0.0).astype(jnp.bfloat16)

    blocks = wide // block
    pieces = [slot_ref[:, k * block : (k + 1) * block] for k in range(blocks)]
    pieces = jnp.concatenate(pieces, axis=0).astype(jnp.float32).astype(jnp.bfloat16)
    moved = jnp.dot(pieces, order[...], preferred_element_type=jnp.float32).astype(jnp.bfloat16)
    for k in range(blocks):
        at = pl.ds(pl.multiple_of((pl.program_id(0) * blocks + k) * lanes, lanes), lanes)
        piece = moved[k * rows : (k + 1) * rows]
        own_ref[:, at] = piece[:, :lanes]
        core_ref[:, at] = piece[:, lanes : 2 * lanes]
        chip_ref[0, :, at] = piece[:, 2 * lanes : 3 * lanes]
        chip_ref[1, :, at] = piece[:, 3 * lanes :]


def slot_parts(bits, slots):
    rows, total = slots.shape
    held = total // 4
    steps = 4 if total >= 64 * rows else 1
    out = jax.ShapeDtypeStruct((rows, held), jnp.bfloat16)
    pair = jax.ShapeDtypeStruct((2, rows, held), jnp.bfloat16)
    return pl.pallas_call(
        slot_kernel,
        grid=(steps,),
        in_specs=[SMEM, pl.BlockSpec((rows, total // steps), lambda s: (0, s))],
        out_specs=[VMEM, VMEM, VMEM],
        out_shape=[out, out, pair],
        scratch_shapes=[pltpu.VMEM((16 * rows, 16 * rows), jnp.bfloat16)],
        compiler_params=params(16),
        name="slot_parts",
    )(bits, slots)


def slots_at(refs, at):
    own, core, chip, both = refs
    return jnp.concatenate([own[:, at], core[:, at], chip[0, :, at], both[1, :, at]], axis=0).astype(jnp.float32)


def score_kernel(tile, group, heat_ref, *refs):
    query_refs, slot_refs = refs[:4], refs[4:8]
    text_ref, stack_ref, e_ref, row_ref, column_ref = refs[8:]
    count, rows, _ = query_refs[0].shape
    images, held = e_ref.shape
    row_ref[...] = jnp.zeros_like(row_ref)
    for q in range(count):
        for member, ref in enumerate(query_refs):
            start = q * images + member * rows
            stack_ref[start : start + rows] = ref[q]

    @pl.loop(0, held // tile)
    def _(step):
        at = pl.ds(pl.multiple_of(step * tile, tile), tile)
        slots = slots_at(slot_refs, at)
        texts = text_ref[at, :]
        picked = jnp.zeros((images, tile), jnp.float32)
        for first in range(0, count, group):
            queries = stack_ref[first * images : (first + group) * images]
            dense = lax.dot_general(
                queries, texts, (((1,), (1,)), ((), ())), preferred_element_type=jnp.float32
            )
            for k in range(group):
                part = dense[k * images : (k + 1) * images]
                picked = jnp.where(slots == float(first + k), part, picked)
        e = jnp.exp(picked * (1.0 / heat_ref[0]))
        e_ref[:, at] = e
        total = jnp.sum(e, axis=0, keepdims=True)
        for k in range(column_ref.shape[0]):
            column_ref[k, :, at] = total
        row_ref[...] += jnp.sum(e, axis=1, keepdims=True)


def scores(copies, heat, queries, slots, texts):
    count, rows, width = queries[0].shape
    held = texts.shape[0]
    images = 4 * rows
    tile = min(512, held)

    def body(*refs):
        score_kernel(tile, 4, *refs)

    return pl.pallas_call(
        body,
        in_specs=[SMEM] + [VMEM] * 9,
        out_specs=[VMEM] * 4,
        out_shape=[
            jax.ShapeDtypeStruct((count * images, width), jnp.bfloat16),
            jax.ShapeDtypeStruct((images, held), jnp.float32),
            jax.ShapeDtypeStruct((images, 1), jnp.float32),
            jax.ShapeDtypeStruct((copies, 1, held), jnp.float32),
        ],
        compiler_params=params(24),
        name="scores",
    )(heat, *queries, *slots, texts)


def column_kernel(column_ref, copies_ref):
    total = jnp.sum(column_ref[...], axis=0, keepdims=True)
    for k in range(copies_ref.shape[0]):
        copies_ref[k] = total


def column_sums(columns, copies):
    held = columns.shape[-1]
    return pl.pallas_call(
        column_kernel,
        in_specs=[VMEM],
        out_specs=VMEM,
        out_shape=jax.ShapeDtypeStruct((copies, 1, held), jnp.float32),
        compiler_params=params(16),
        name="column_sums",
    )(columns.reshape(-1, held))


def row_totals(row_refs):
    rows = row_refs[0].shape[0] // 4
    members = []
    for member in range(4):
        parts = [ref[(member ^ k) * rows : ((member ^ k) + 1) * rows] for k, ref in enumerate(row_refs)]
        members.append((parts[0] + parts[1]) + (parts[2] + parts[3]))
    return jnp.concatenate(members, axis=0)


def score_gradient(total, heat_ref, e, row, columns, target):
    half = 0.5 * (1.0 / heat_ref[0])
    column = jnp.sum(columns, axis=0)
    return (e / row - target) * half + (e / column - target) * half


def text_grad_kernel(total, heat_ref, first_ref, stack_ref, *refs):
    slot_refs, row_refs, (e_ref, column_ref, dt_ref, mark_ref, mix) = refs[:4], refs[4:8], refs[8:]
    images = e_ref.shape[0]
    tile, depth = mix.shape
    start = pl.multiple_of(pl.program_id(0) * tile, tile)
    at = pl.ds(start, tile)
    image = lax.broadcasted_iota(jnp.int32, (images, tile), 0)
    text = lax.broadcasted_iota(jnp.int32, (images, tile), 1) + (start - first_ref[0])
    g = score_gradient(total, heat_ref, e_ref[:, at], row_totals(row_refs), column_ref[:, :, at], 0.1 / total)
    g = jnp.where((image == text) & (image < images // 4), 0.0, g).T
    slots = slots_at(slot_refs, at).T
    for q in range(depth // images):
        mix[:, q * images : (q + 1) * images] = jnp.where(slots == float(q), g, 0.0).astype(jnp.bfloat16)
    dt_ref[...] = jnp.dot(mix[...], stack_ref[...], preferred_element_type=jnp.float32) * SENT
    mark_ref[...] = dt_ref[:8, :LANES]


def text_gradients(total, heat, first, stack, slots, rows, e, column):
    depth, width = stack.shape
    held = e.shape[1]
    tile = min(512, held)

    def body(*refs):
        text_grad_kernel(total, *refs)

    return pl.pallas_call(
        body,
        grid=(held // tile,),
        in_specs=[SMEM, SMEM] + [VMEM] * 11,
        out_specs=[pl.BlockSpec((tile, width), lambda s: (s, 0)), VMEM],
        out_shape=[
            jax.ShapeDtypeStruct((held, width), jnp.float32),
            jax.ShapeDtypeStruct((8, LANES), jnp.float32),
        ],
        scratch_shapes=[pltpu.VMEM((tile, depth), jnp.bfloat16)],
        compiler_params=params(28),
        name="text_gradients",
    )(heat, first, stack, *slots, *rows, e, column)


def query_grad_kernel(total, heat_ref, mark_ref, *refs):
    slot_refs, row_refs, (text_ref, e_ref, column_ref), outs, mix = refs[:4], refs[4:8], refs[8:11], refs[11:14], refs[14]
    count, rows, _ = outs[0].shape
    images = 3 * rows
    group = mix.shape[0] // images
    slots = slots_at(slot_refs, slice(None))[rows:]
    row = row_totals(row_refs)[rows:]
    g = score_gradient(total, heat_ref, e_ref[rows:], row, column_ref[...], 0.1 / total)
    texts = text_ref[...]
    for first in range(0, count, group):
        for k in range(group):
            kept = jnp.where(slots == float(first + k), g, 0.0)
            mix[k * images : (k + 1) * images] = kept.astype(jnp.bfloat16)
        part = jnp.dot(mix[...], texts, preferred_element_type=jnp.float32)
        for k in range(group):
            for member, out in enumerate(outs):
                at = k * images + member * rows
                out[first + k] = part[at : at + rows]


def query_gradients(total, count, heat, mark, slots, row_parts, texts, e, column):
    images, held = e.shape
    rows = images // 4
    width = texts.shape[1]
    group = 8

    def body(*refs):
        query_grad_kernel(total, *refs)

    return pl.pallas_call(
        body,
        in_specs=[SMEM, pl.BlockSpec(memory_space=pl.ANY)] + [VMEM] * 11,
        out_specs=[VMEM] * 3,
        out_shape=[jax.ShapeDtypeStruct((count, rows, width), jnp.float32)] * 3,
        scratch_shapes=[pltpu.VMEM((group * 3 * rows, held), jnp.bfloat16)],
        compiler_params=params(28),
        name="query_gradients",
    )(heat, mark, *slots, *row_parts, texts, e, column)


def finish_kernel(total, heat_ref, first_ref, probe_ref, slot_ref, *refs):
    row_refs, (text_ref, e_ref, column_ref, core_ref, chip_ref, out_ref, pair_ref, mix, sums, pair_mix, half) = refs[:4], refs[4:]
    block, count, width = probe_ref.shape
    held = e_ref.shape[1]
    start = pl.multiple_of(pl.program_id(0) * block, block)
    here = pl.ds(start, block)
    rows = slot_ref.shape[0]
    row = sum(ref[pl.ds(k * rows + start, block), :] for k, ref in enumerate(row_refs))
    image = lax.broadcasted_iota(jnp.int32, (block, held), 0) + start
    text = lax.broadcasted_iota(jnp.int32, (block, held), 1) - first_ref[0]
    matched = image == text
    target = jnp.where(matched, 0.9, 0.0) + 0.1 / total
    g = score_gradient(total, heat_ref, e_ref[here, :], row, column_ref[...], target)
    slots = slot_ref[here, :].astype(jnp.float32)
    pair_g = jnp.sum(jnp.where(matched, g, 0.0), axis=1, keepdims=True)
    pair_slot = jnp.sum(jnp.where(matched, slots, 0.0), axis=1, keepdims=True)
    query = lax.broadcasted_iota(jnp.int32, (count, 1), 0).astype(jnp.float32)
    pair_mix[...] = jnp.broadcast_to(pair_g, pair_mix.shape).astype(jnp.bfloat16)
    pair_g = pair_mix[...].astype(jnp.float32)[:, :1]
    for q in range(count):
        mix[q * block : (q + 1) * block] = jnp.where(slots == float(q), g, 0.0).astype(jnp.bfloat16)
    added = jnp.dot(mix[...], text_ref[...], preferred_element_type=jnp.float32)
    added += (core_ref[:, here, :] + chip_ref[:, here, :].astype(jnp.float32)).reshape(count * block, width)
    halves = range(width // LANES)
    for k in halves:
        sums[k] = added[:, k * LANES : (k + 1) * LANES]
    for i in range(block):
        unit, scale = normalized_rows(probe_ref[i])
        half[i] = unit.astype(jnp.bfloat16)
        pair = jnp.where(query == pair_slot[i : i + 1], pair_g[i : i + 1], 0.0)
        pair_ref[i : i + 1, :] = jnp.sum(pair * half[i].astype(jnp.float32), axis=0, keepdims=True)
        dq = jnp.concatenate([sums[k, pl.ds(i, count, stride=block), :] for k in halves], axis=1)
        out_ref[i] = (dq - unit * jnp.sum(unit * dq, axis=-1, keepdims=True)) * scale


def finish_queries(total, heat, first, probes, slots, row_parts, texts, e, column, core, chip):
    rows, count, width = probes.shape
    block = min(16, rows)
    kept = pl.BlockSpec((block, count, width), lambda s: (s, 0, 0))

    def body(*refs):
        finish_kernel(total, *refs)

    return pl.pallas_call(
        body,
        grid=(rows // block,),
        in_specs=[SMEM, SMEM, kept] + [VMEM] * 10,
        out_specs=[kept, pl.BlockSpec((block, width), lambda s: (s, 0))],
        out_shape=[
            jax.ShapeDtypeStruct(probes.shape, jnp.float32),
            jax.ShapeDtypeStruct((rows, width), jnp.float32),
        ],
        scratch_shapes=[
            pltpu.VMEM((count * block, e.shape[1]), jnp.bfloat16),
            pltpu.VMEM((width // LANES, count * block, LANES), jnp.float32),
            pltpu.VMEM((block, LANES), jnp.bfloat16),
            pltpu.VMEM((block, count, width), jnp.bfloat16),
        ],
        compiler_params=params(24),
        name="finish_queries",
    )(heat, first, probes, slots, *row_parts, texts, e, column, core, chip)


def finish_text_kernel(caption_ref, block_ref, pair_ref, out_ref):
    unit, scale = normalized_rows(caption_ref[...])
    dt = jnp.sum(block_ref[...], axis=0) * (1.0 / SENT) + pair_ref[...]
    out_ref[...] = (dt - unit * jnp.sum(unit * dt, axis=-1, keepdims=True)) * scale


def finish_texts(captions, blocks, pairs):
    return pl.pallas_call(
        finish_text_kernel,
        in_specs=[VMEM] * 3,
        out_specs=VMEM,
        out_shape=jax.ShapeDtypeStruct(captions.shape, jnp.float32),
        compiler_params=params(16),
        name="finish_texts",
    )(captions, blocks, pairs)


def swap_z(values):
    return lax.ppermute(values, "zp", SWAP)


def swap_c(values):
    return lax.ppermute(values, "c", SWAP)


def shards(picture_probes, caption_vectors, chosen_slot_per_match, softmax_heat):
    rows, count, width = picture_probes.shape
    total = chosen_slot_per_match.shape[1]
    held = total // 4
    groups, outer = lax.axis_size("dp"), lax.axis_size("zo")

    texts = lax.all_to_all(half_texts(caption_vectors, outer), "zo", 0, 0, tiled=True)
    texts = jnp.broadcast_to(texts.reshape(1, outer * rows, width), (groups, outer * rows, width))
    texts = lax.all_to_all(texts, "dp", 0, 0, tiled=True).reshape(held, width)

    bits = (lax.axis_index("zp") * 2 + lax.axis_index("c")).astype(jnp.int32).reshape(1)
    q_own = half_queries(picture_probes)
    slots_own, slots_core, slots_chip = slot_parts(bits, chosen_slot_per_match)
    q_chip = swap_z(q_own)
    slots_chip = swap_z(slots_chip)
    queries = (q_own, swap_c(q_own), q_chip, swap_c(q_chip))
    slots = (slots_own, swap_c(slots_core), slots_chip, swap_c(slots_chip))

    stack, e, row, column = scores(groups, softmax_heat, queries, slots, texts)

    row_chip = swap_z(row)
    row_parts = (row, swap_c(row), row_chip, swap_c(row_chip))
    column = lax.all_to_all(column, "dp", 0, 0, tiled=True)
    column = lax.all_to_all(column_sums(column, outer), "zo", 0, 0, tiled=True)

    place = lax.axis_index("dp") * outer + lax.axis_index("zo")
    first = (place * rows).astype(jnp.int32).reshape(1)
    dt, mark = text_gradients(total, softmax_heat, first, stack, slots, row_parts, e, column)
    dt = lax.all_to_all(dt.astype(HALF).reshape(groups, outer * rows, width), "dp", 0, 0, tiled=True)
    common = (row_parts, texts, e, column)
    dq_core, dq_chip, dq_both = query_gradients(total, count, softmax_heat, mark, slots, *common)
    dq_chip = dq_chip + swap_c(dq_both.astype(HALF)).astype(jnp.float32)
    dq_chip = swap_z(dq_chip.astype(HALF)).astype(jnp.float32)
    dq_core = swap_c(dq_core)
    dt = jnp.sum(dt.astype(jnp.float32), axis=0).reshape(outer, rows, width)
    dt = lax.all_to_all(dt, "zo", 0, 0, tiled=True)
    query_grads, pairs = finish_queries(
        total, softmax_heat, first, picture_probes, slots[0], *common, dq_core, dq_chip
    )
    text_grads = finish_texts(caption_vectors, dt, pairs)
    return (query_grads, text_grads)


def solution(mesh):
    groups, replicas = mesh.devices.shape
    axes = ("dp", "zo", "zp", "c")
    split = Mesh(mesh.devices.reshape(groups, replicas // 4, 2, 2), axes)
    return jax.shard_map(
        shards,
        mesh=split,
        in_specs=(P(axes, None, None), P(axes, None), P(axes, None), P()),
        out_specs=(P(axes, None, None), P(axes, None)),
        check_vma=False,
    )
```

```python
import jax
import jax.numpy as jnp
from jax import lax
from jax.experimental import pallas as pl
from jax.experimental.pallas import tpu as pltpu
from jax.sharding import Mesh
from jax.sharding import PartitionSpec as P

EPS = 1e-06
LANES = 128
HALF = jnp.float16
SENT = 16.0
SWAP = [(0, 1), (1, 0)]
SMEM = pl.BlockSpec(memory_space=pltpu.SMEM)
VMEM = pl.BlockSpec(memory_space=pltpu.VMEM)


def params(mib):
    return pltpu.CompilerParams(vmem_limit_bytes=mib * 1024 * 1024)


def normalized_rows(values):
    wide = values.astype(jnp.float32)
    scale = lax.rsqrt(jnp.sum(wide * wide, axis=-1, keepdims=True) + EPS)
    return (wide * scale, scale)


def text_kernel(caption_ref, copies_ref):
    unit, _ = normalized_rows(caption_ref[...])
    half = unit.astype(jnp.bfloat16)
    for k in range(copies_ref.shape[0]):
        copies_ref[k] = half


def half_texts(captions, copies):
    return pl.pallas_call(
        text_kernel,
        in_specs=[VMEM],
        out_specs=VMEM,
        out_shape=jax.ShapeDtypeStruct((copies, *captions.shape), jnp.bfloat16),
        compiler_params=params(16),
        name="half_texts",
    )(captions)


def query_kernel(probe_ref, half_ref, units):
    rows, count, width = probe_ref.shape
    unit, _ = normalized_rows(probe_ref[...])
    unit = unit.reshape(rows * count, width)
    here = pl.ds(pl.multiple_of(pl.program_id(0) * rows, rows), rows)
    for k in range(width // LANES):
        at = slice(k * LANES, (k + 1) * LANES)
        units[k, : rows * count] = unit[:, at]
        for q in range(count):
            half_ref[q, here, at] = units[k, pl.ds(q, rows, stride=count), :].astype(jnp.bfloat16)


def half_queries(probes):
    rows, count, width = probes.shape
    block = min(16, rows)
    return pl.pallas_call(
        query_kernel,
        grid=(rows // block,),
        in_specs=[pl.BlockSpec((block, count, width), lambda s: (s, 0, 0))],
        out_specs=VMEM,
        out_shape=jax.ShapeDtypeStruct((count, rows, width), jnp.bfloat16),
        scratch_shapes=[pltpu.VMEM((width // LANES, (block + 1) * count, LANES), jnp.float32)],
        compiler_params=params(16),
        name="half_queries",
    )(probes)


def slot_kernel(bits_ref, slot_ref, own_ref, core_ref, chip_ref, order):
    rows, wide = slot_ref.shape
    lanes = 4 * rows
    block = 4 * lanes

    @pl.when(pl.program_id(0) == 0)
    def _():
        source = lax.broadcasted_iota(jnp.int32, (block, block), 0)
        goal = lax.broadcasted_iota(jnp.int32, (1, block), 1)
        member = (goal // lanes) ^ bits_ref[0]
        wanted = (goal % lanes) // rows * lanes + member * rows + goal % rows
        order[...] = jnp.where(source == wanted, 1.0, 0.0).astype(jnp.bfloat16)

    blocks = wide // block
    pieces = [slot_ref[:, k * block : (k + 1) * block] for k in range(blocks)]
    pieces = jnp.concatenate(pieces, axis=0).astype(jnp.float32).astype(jnp.bfloat16)
    moved = jnp.dot(pieces, order[...], preferred_element_type=jnp.float32).astype(jnp.bfloat16)
    for k in range(blocks):
        at = pl.ds(pl.multiple_of((pl.program_id(0) * blocks + k) * lanes, lanes), lanes)
        piece = moved[k * rows : (k + 1) * rows]
        own_ref[:, at] = piece[:, :lanes]
        core_ref[:, at] = piece[:, lanes : 2 * lanes]
        chip_ref[0, :, at] = piece[:, 2 * lanes : 3 * lanes]
        chip_ref[1, :, at] = piece[:, 3 * lanes :]


def slot_parts(bits, slots):
    rows, total = slots.shape
    held = total // 4
    steps = 4 if total >= 64 * rows else 1
    out = jax.ShapeDtypeStruct((rows, held), jnp.bfloat16)
    pair = jax.ShapeDtypeStruct((2, rows, held), jnp.bfloat16)
    return pl.pallas_call(
        slot_kernel,
        grid=(steps,),
        in_specs=[SMEM, pl.BlockSpec((rows, total // steps), lambda s: (0, s))],
        out_specs=[VMEM, VMEM, VMEM],
        out_shape=[out, out, pair],
        scratch_shapes=[pltpu.VMEM((16 * rows, 16 * rows), jnp.bfloat16)],
        compiler_params=params(16),
        name="slot_parts",
    )(bits, slots)


def slots_at(refs, at):
    own, core, chip, both = refs
    return jnp.concatenate([own[:, at], core[:, at], chip[0, :, at], both[1, :, at]], axis=0).astype(jnp.float32)


def score_kernel(tile, group, heat_ref, *refs):
    query_refs, slot_refs = refs[:4], refs[4:8]
    text_ref, stack_ref, e_ref, row_ref, column_ref = refs[8:]
    count, rows, _ = query_refs[0].shape
    images, held = e_ref.shape
    row_ref[...] = jnp.zeros_like(row_ref)
    for q in range(count):
        for member, ref in enumerate(query_refs):
            start = q * images + member * rows
            stack_ref[start : start + rows] = ref[q]

    @pl.loop(0, held // tile)
    def _(step):
        at = pl.ds(pl.multiple_of(step * tile, tile), tile)
        slots = slots_at(slot_refs, at)
        texts = text_ref[at, :]
        picked = jnp.zeros((images, tile), jnp.float32)
        for first in range(0, count, group):
            queries = stack_ref[first * images : (first + group) * images]
            dense = lax.dot_general(
                queries, texts, (((1,), (1,)), ((), ())), preferred_element_type=jnp.float32
            )
            for k in range(group):
                part = dense[k * images : (k + 1) * images]
                picked = jnp.where(slots == float(first + k), part, picked)
        e = jnp.exp(picked * (1.0 / heat_ref[0]))
        e_ref[:, at] = e
        total = jnp.sum(e, axis=0, keepdims=True)
        for k in range(column_ref.shape[0]):
            column_ref[k, :, at] = total
        row_ref[...] += jnp.sum(e, axis=1, keepdims=True)


def scores(copies, heat, queries, slots, texts):
    count, rows, width = queries[0].shape
    held = texts.shape[0]
    images = 4 * rows
    tile = min(512, held)

    def body(*refs):
        score_kernel(tile, 4, *refs)

    return pl.pallas_call(
        body,
        in_specs=[SMEM] + [VMEM] * 9,
        out_specs=[VMEM] * 4,
        out_shape=[
            jax.ShapeDtypeStruct((count * images, width), jnp.bfloat16),
            jax.ShapeDtypeStruct((images, held), jnp.float32),
            jax.ShapeDtypeStruct((images, 1), jnp.float32),
            jax.ShapeDtypeStruct((copies, 1, held), jnp.float32),
        ],
        compiler_params=params(24),
        name="scores",
    )(heat, *queries, *slots, texts)


def column_kernel(column_ref, copies_ref):
    total = jnp.sum(column_ref[...], axis=0, keepdims=True)
    for k in range(copies_ref.shape[0]):
        copies_ref[k] = total


def column_sums(columns, copies):
    held = columns.shape[-1]
    return pl.pallas_call(
        column_kernel,
        in_specs=[VMEM],
        out_specs=VMEM,
        out_shape=jax.ShapeDtypeStruct((copies, 1, held), jnp.float32),
        compiler_params=params(16),
        name="column_sums",
    )(columns.reshape(-1, held))


def row_totals(row_refs):
    rows = row_refs[0].shape[0] // 4
    members = []
    for member in range(4):
        parts = [ref[(member ^ k) * rows : ((member ^ k) + 1) * rows] for k, ref in enumerate(row_refs)]
        members.append((parts[0] + parts[1]) + (parts[2] + parts[3]))
    return jnp.concatenate(members, axis=0)


def score_gradient(total, heat_ref, e, row, columns, target):
    half = 0.5 * (1.0 / heat_ref[0])
    column = jnp.sum(columns, axis=0)
    return (e / row - target) * half + (e / column - target) * half


def text_grad_kernel(total, heat_ref, first_ref, stack_ref, *refs):
    slot_refs, row_refs, (e_ref, column_ref, dt_ref, mark_ref, mix) = refs[:4], refs[4:8], refs[8:]
    images = e_ref.shape[0]
    tile, depth = mix.shape
    start = pl.multiple_of(pl.program_id(0) * tile, tile)
    at = pl.ds(start, tile)
    image = lax.broadcasted_iota(jnp.int32, (images, tile), 0)
    text = lax.broadcasted_iota(jnp.int32, (images, tile), 1) + (start - first_ref[0])
    g = score_gradient(total, heat_ref, e_ref[:, at], row_totals(row_refs), column_ref[:, :, at], 0.1 / total)
    g = jnp.where((image == text) & (image < images // 4), 0.0, g).T
    slots = slots_at(slot_refs, at).T
    for q in range(depth // images):
        mix[:, q * images : (q + 1) * images] = jnp.where(slots == float(q), g, 0.0).astype(jnp.bfloat16)
    dt_ref[...] = jnp.dot(mix[...], stack_ref[...], preferred_element_type=jnp.float32) * SENT
    mark_ref[...] = dt_ref[:8, :LANES]


def text_gradients(total, heat, first, stack, slots, rows, e, column):
    depth, width = stack.shape
    held = e.shape[1]
    tile = min(512, held)

    def body(*refs):
        text_grad_kernel(total, *refs)

    return pl.pallas_call(
        body,
        grid=(held // tile,),
        in_specs=[SMEM, SMEM] + [VMEM] * 11,
        out_specs=[pl.BlockSpec((tile, width), lambda s: (s, 0)), VMEM],
        out_shape=[
            jax.ShapeDtypeStruct((held, width), jnp.float32),
            jax.ShapeDtypeStruct((8, LANES), jnp.float32),
        ],
        scratch_shapes=[pltpu.VMEM((tile, depth), jnp.bfloat16)],
        compiler_params=params(28),
        name="text_gradients",
    )(heat, first, stack, *slots, *rows, e, column)


def query_grad_kernel(total, heat_ref, mark_ref, *refs):
    slot_refs, row_refs, (text_ref, e_ref, column_ref), outs, mix = refs[:4], refs[4:8], refs[8:11], refs[11:14], refs[14]
    count, rows, _ = outs[0].shape
    images = 3 * rows
    group = mix.shape[0] // images
    slots = slots_at(slot_refs, slice(None))[rows:]
    row = row_totals(row_refs)[rows:]
    g = score_gradient(total, heat_ref, e_ref[rows:], row, column_ref[...], 0.1 / total)
    texts = text_ref[...]
    for first in range(0, count, group):
        for k in range(group):
            kept = jnp.where(slots == float(first + k), g, 0.0)
            mix[k * images : (k + 1) * images] = kept.astype(jnp.bfloat16)
        part = jnp.dot(mix[...], texts, preferred_element_type=jnp.float32)
        for k in range(group):
            for member, out in enumerate(outs):
                at = k * images + member * rows
                out[first + k] = part[at : at + rows]


def query_gradients(total, count, heat, mark, slots, row_parts, texts, e, column):
    images, held = e.shape
    rows = images // 4
    width = texts.shape[1]
    group = 8

    def body(*refs):
        query_grad_kernel(total, *refs)

    return pl.pallas_call(
        body,
        in_specs=[SMEM, pl.BlockSpec(memory_space=pl.ANY)] + [VMEM] * 11,
        out_specs=[VMEM] * 3,
        out_shape=[jax.ShapeDtypeStruct((count, rows, width), jnp.float32)] * 3,
        scratch_shapes=[pltpu.VMEM((group * 3 * rows, held), jnp.bfloat16)],
        compiler_params=params(28),
        name="query_gradients",
    )(heat, mark, *slots, *row_parts, texts, e, column)


def finish_kernel(total, heat_ref, first_ref, probe_ref, slot_ref, *refs):
    row_refs, (text_ref, e_ref, column_ref, core_ref, chip_ref, out_ref, pair_ref, mix, sums, pair_mix, half) = refs[:4], refs[4:]
    block, count, width = probe_ref.shape
    held = e_ref.shape[1]
    start = pl.multiple_of(pl.program_id(0) * block, block)
    here = pl.ds(start, block)
    rows = slot_ref.shape[0]
    row = sum(ref[pl.ds(k * rows + start, block), :] for k, ref in enumerate(row_refs))
    image = lax.broadcasted_iota(jnp.int32, (block, held), 0) + start
    text = lax.broadcasted_iota(jnp.int32, (block, held), 1) - first_ref[0]
    matched = image == text
    target = jnp.where(matched, 0.9, 0.0) + 0.1 / total
    g = score_gradient(total, heat_ref, e_ref[here, :], row, column_ref[...], target)
    slots = slot_ref[here, :].astype(jnp.float32)
    pair_g = jnp.sum(jnp.where(matched, g, 0.0), axis=1, keepdims=True)
    pair_slot = jnp.sum(jnp.where(matched, slots, 0.0), axis=1, keepdims=True)
    query = lax.broadcasted_iota(jnp.int32, (count, 1), 0).astype(jnp.float32)
    pair_mix[...] = jnp.broadcast_to(pair_g, pair_mix.shape).astype(jnp.bfloat16)
    pair_g = pair_mix[...].astype(jnp.float32)[:, :1]
    for q in range(count):
        mix[q * block : (q + 1) * block] = jnp.where(slots == float(q), g, 0.0).astype(jnp.bfloat16)
    added = jnp.dot(mix[...], text_ref[...], preferred_element_type=jnp.float32)
    added += (core_ref[:, here, :] + chip_ref[:, here, :].astype(jnp.float32)).reshape(count * block, width)
    halves = range(width // LANES)
    for k in halves:
        sums[k, : count * block] = added[:, k * LANES : (k + 1) * LANES]
    for i in range(block):
        unit, scale = normalized_rows(probe_ref[i])
        half[i] = unit.astype(jnp.bfloat16)
        pair = jnp.where(query == pair_slot[i : i + 1], pair_g[i : i + 1], 0.0)
        pair_ref[i : i + 1, :] = jnp.sum(pair * half[i].astype(jnp.float32), axis=0, keepdims=True)
        dq = jnp.concatenate([sums[k, pl.ds(i, count, stride=block), :] for k in halves], axis=1)
        out_ref[i] = (dq - unit * jnp.sum(unit * dq, axis=-1, keepdims=True)) * scale


def finish_queries(total, heat, first, probes, slots, row_parts, texts, e, column, core, chip):
    rows, count, width = probes.shape
    block = min(16, rows)
    kept = pl.BlockSpec((block, count, width), lambda s: (s, 0, 0))

    def body(*refs):
        finish_kernel(total, *refs)

    return pl.pallas_call(
        body,
        grid=(rows // block,),
        in_specs=[SMEM, SMEM, kept] + [VMEM] * 10,
        out_specs=[kept, pl.BlockSpec((block, width), lambda s: (s, 0))],
        out_shape=[
            jax.ShapeDtypeStruct(probes.shape, jnp.float32),
            jax.ShapeDtypeStruct((rows, width), jnp.float32),
        ],
        scratch_shapes=[
            pltpu.VMEM((count * block, e.shape[1]), jnp.bfloat16),
            pltpu.VMEM((width // LANES, (count + 1) * block, LANES), jnp.float32),
            pltpu.VMEM((block, LANES), jnp.bfloat16),
            pltpu.VMEM((block, count, width), jnp.bfloat16),
        ],
        compiler_params=params(24),
        name="finish_queries",
    )(heat, first, probes, slots, *row_parts, texts, e, column, core, chip)


def finish_text_kernel(caption_ref, block_ref, pair_ref, out_ref):
    unit, scale = normalized_rows(caption_ref[...])
    dt = jnp.sum(block_ref[...], axis=0) * (1.0 / SENT) + pair_ref[...]
    out_ref[...] = (dt - unit * jnp.sum(unit * dt, axis=-1, keepdims=True)) * scale


def finish_texts(captions, blocks, pairs):
    return pl.pallas_call(
        finish_text_kernel,
        in_specs=[VMEM] * 3,
        out_specs=VMEM,
        out_shape=jax.ShapeDtypeStruct(captions.shape, jnp.float32),
        compiler_params=params(16),
        name="finish_texts",
    )(captions, blocks, pairs)


def swap_z(values):
    return lax.ppermute(values, "zp", SWAP)


def swap_c(values):
    return lax.ppermute(values, "c", SWAP)


def shards(picture_probes, caption_vectors, chosen_slot_per_match, softmax_heat):
    rows, count, width = picture_probes.shape
    total = chosen_slot_per_match.shape[1]
    held = total // 4
    groups, outer = lax.axis_size("dp"), lax.axis_size("zo")

    texts = lax.all_to_all(half_texts(caption_vectors, outer), "zo", 0, 0, tiled=True)
    texts = jnp.broadcast_to(texts.reshape(1, outer * rows, width), (groups, outer * rows, width))
    texts = lax.all_to_all(texts, "dp", 0, 0, tiled=True).reshape(held, width)

    bits = (lax.axis_index("zp") * 2 + lax.axis_index("c")).astype(jnp.int32).reshape(1)
    q_own = half_queries(picture_probes)
    slots_own, slots_core, slots_chip = slot_parts(bits, chosen_slot_per_match)
    q_chip = swap_z(q_own)
    slots_chip = swap_z(slots_chip)
    queries = (q_own, swap_c(q_own), q_chip, swap_c(q_chip))
    slots = (slots_own, swap_c(slots_core), slots_chip, swap_c(slots_chip))

    stack, e, row, column = scores(groups, softmax_heat, queries, slots, texts)

    row_chip = swap_z(row)
    row_parts = (row, swap_c(row), row_chip, swap_c(row_chip))
    column = lax.all_to_all(column, "dp", 0, 0, tiled=True)
    column = lax.all_to_all(column_sums(column, outer), "zo", 0, 0, tiled=True)

    place = lax.axis_index("dp") * outer + lax.axis_index("zo")
    first = (place * rows).astype(jnp.int32).reshape(1)
    dt, mark = text_gradients(total, softmax_heat, first, stack, slots, row_parts, e, column)
    dt = lax.all_to_all(dt.astype(HALF).reshape(groups, outer * rows, width), "dp", 0, 0, tiled=True)
    common = (row_parts, texts, e, column)
    dq_core, dq_chip, dq_both = query_gradients(total, count, softmax_heat, mark, slots, *common)
    dq_chip = dq_chip + swap_c(dq_both.astype(HALF)).astype(jnp.float32)
    dq_chip = swap_z(dq_chip.astype(HALF)).astype(jnp.float32)
    dq_core = swap_c(dq_core)
    dt = jnp.sum(dt.astype(jnp.float32), axis=0).reshape(outer, rows, width)
    dt = lax.all_to_all(dt, "zo", 0, 0, tiled=True)
    query_grads, pairs = finish_queries(
        total, softmax_heat, first, picture_probes, slots[0], *common, dq_core, dq_chip
    )
    text_grads = finish_texts(caption_vectors, dt, pairs)
    return (query_grads, text_grads)


def solution(mesh):
    groups, replicas = mesh.devices.shape
    axes = ("dp", "zo", "zp", "c")
    split = Mesh(mesh.devices.reshape(groups, replicas // 4, 2, 2), axes)
    return jax.shard_map(
        shards,
        mesh=split,
        in_specs=(P(axes, None, None), P(axes, None), P(axes, None), P()),
        out_specs=(P(axes, None, None), P(axes, None)),
        check_vma=False,
    )
```

```python
import jax
import jax.numpy as jnp
from jax import lax
from jax.experimental import pallas as pl
from jax.experimental.pallas import tpu as pltpu
from jax.sharding import Mesh
from jax.sharding import PartitionSpec as P

EPS = 1e-06
LANES = 128
HALF = jnp.float16
SENT = 16.0
SWAP = [(0, 1), (1, 0)]
SMEM = pl.BlockSpec(memory_space=pltpu.SMEM)
VMEM = pl.BlockSpec(memory_space=pltpu.VMEM)


def params(mib):
    return pltpu.CompilerParams(vmem_limit_bytes=mib * 1024 * 1024)


def normalized_rows(values):
    wide = values.astype(jnp.float32)
    scale = lax.rsqrt(jnp.sum(wide * wide, axis=-1, keepdims=True) + EPS)
    return (wide * scale, scale)


def text_kernel(caption_ref, copies_ref):
    unit, _ = normalized_rows(caption_ref[...])
    half = unit.astype(jnp.bfloat16)
    for k in range(copies_ref.shape[0]):
        copies_ref[k] = half


def half_texts(captions, copies):
    return pl.pallas_call(
        text_kernel,
        in_specs=[VMEM],
        out_specs=VMEM,
        out_shape=jax.ShapeDtypeStruct((copies, *captions.shape), jnp.bfloat16),
        compiler_params=params(16),
        name="half_texts",
    )(captions)


def query_kernel(probe_ref, half_ref, units):
    rows, count, width = probe_ref.shape
    unit, _ = normalized_rows(probe_ref[...])
    unit = unit.reshape(rows * count, width)
    here = pl.ds(pl.multiple_of(pl.program_id(0) * rows, rows), rows)
    for k in range(width // LANES):
        at = slice(k * LANES, (k + 1) * LANES)
        units[k, : rows * count] = unit[:, at]
        for q in range(count):
            half_ref[q, here, at] = units[k, pl.ds(q, rows, stride=count), :].astype(jnp.bfloat16)


def half_queries(probes):
    rows, count, width = probes.shape
    block = min(16, rows)
    return pl.pallas_call(
        query_kernel,
        grid=(rows // block,),
        in_specs=[pl.BlockSpec((block, count, width), lambda s: (s, 0, 0))],
        out_specs=VMEM,
        out_shape=jax.ShapeDtypeStruct((count, rows, width), jnp.bfloat16),
        scratch_shapes=[pltpu.VMEM((width // LANES, (block + 1) * count, LANES), jnp.float32)],
        compiler_params=params(16),
        name="half_queries",
    )(probes)


def slot_kernel(bits_ref, slot_ref, own_ref, core_ref, chip_ref, order):
    rows, wide = slot_ref.shape
    lanes = 4 * rows
    block = 4 * lanes

    @pl.when(pl.program_id(0) == 0)
    def _():
        source = lax.broadcasted_iota(jnp.int32, (block, block), 0)
        goal = lax.broadcasted_iota(jnp.int32, (1, block), 1)
        member = (goal // lanes) ^ bits_ref[0]
        wanted = (goal % lanes) // rows * lanes + member * rows + goal % rows
        order[...] = jnp.where(source == wanted, 1.0, 0.0).astype(jnp.bfloat16)

    blocks = wide // block
    pieces = [slot_ref[:, k * block : (k + 1) * block] for k in range(blocks)]
    pieces = jnp.concatenate(pieces, axis=0).astype(jnp.float32).astype(jnp.bfloat16)
    moved = jnp.dot(pieces, order[...], preferred_element_type=jnp.float32).astype(jnp.bfloat16)
    for k in range(blocks):
        at = pl.ds(pl.multiple_of((pl.program_id(0) * blocks + k) * lanes, lanes), lanes)
        piece = moved[k * rows : (k + 1) * rows]
        own_ref[:, at] = piece[:, :lanes]
        core_ref[:, at] = piece[:, lanes : 2 * lanes]
        chip_ref[0, :, at] = piece[:, 2 * lanes : 3 * lanes]
        chip_ref[1, :, at] = piece[:, 3 * lanes :]


def slot_parts(bits, slots):
    rows, total = slots.shape
    held = total // 4
    steps = 4 if total >= 64 * rows else 1
    out = jax.ShapeDtypeStruct((rows, held), jnp.bfloat16)
    pair = jax.ShapeDtypeStruct((2, rows, held), jnp.bfloat16)
    return pl.pallas_call(
        slot_kernel,
        grid=(steps,),
        in_specs=[SMEM, pl.BlockSpec((rows, total // steps), lambda s: (0, s))],
        out_specs=[VMEM, VMEM, VMEM],
        out_shape=[out, out, pair],
        scratch_shapes=[pltpu.VMEM((16 * rows, 16 * rows), jnp.bfloat16)],
        compiler_params=params(16),
        name="slot_parts",
    )(bits, slots)


def slots_at(refs, at):
    own, core, chip, both = refs
    return jnp.concatenate([own[:, at], core[:, at], chip[0, :, at], both[1, :, at]], axis=0).astype(jnp.float32)


def score_kernel(tile, group, heat_ref, *refs):
    query_refs, slot_refs = refs[:4], refs[4:8]
    text_ref, stack_ref, e_ref, row_ref, column_ref = refs[8:]
    count, rows, _ = query_refs[0].shape
    images, held = e_ref.shape
    row_ref[...] = jnp.zeros_like(row_ref)
    for q in range(count):
        for member, ref in enumerate(query_refs):
            start = q * images + member * rows
            stack_ref[start : start + rows] = ref[q]

    @pl.loop(0, held // tile)
    def _(step):
        at = pl.ds(pl.multiple_of(step * tile, tile), tile)
        slots = slots_at(slot_refs, at)
        texts = text_ref[at, :]
        picked = jnp.zeros((images, tile), jnp.float32)
        for first in range(0, count, group):
            queries = stack_ref[first * images : (first + group) * images]
            dense = lax.dot_general(
                queries, texts, (((1,), (1,)), ((), ())), preferred_element_type=jnp.float32
            )
            for k in range(group):
                part = dense[k * images : (k + 1) * images]
                picked = jnp.where(slots == float(first + k), part, picked)
        e = jnp.exp(picked * (1.0 / heat_ref[0]))
        e_ref[:, at] = e
        total = jnp.sum(e, axis=0, keepdims=True)
        for k in range(column_ref.shape[0]):
            column_ref[k, :, at] = total
        row_ref[...] += jnp.sum(e, axis=1, keepdims=True)


def scores(copies, heat, queries, slots, texts):
    count, rows, width = queries[0].shape
    held = texts.shape[0]
    images = 4 * rows
    tile = min(1024, held)

    def body(*refs):
        score_kernel(tile, 4, *refs)

    return pl.pallas_call(
        body,
        in_specs=[SMEM] + [VMEM] * 9,
        out_specs=[VMEM] * 4,
        out_shape=[
            jax.ShapeDtypeStruct((count * images, width), jnp.bfloat16),
            jax.ShapeDtypeStruct((images, held), jnp.float32),
            jax.ShapeDtypeStruct((images, 1), jnp.float32),
            jax.ShapeDtypeStruct((copies, 1, held), jnp.float32),
        ],
        compiler_params=params(24),
        name="scores",
    )(heat, *queries, *slots, texts)


def column_kernel(column_ref, copies_ref):
    total = jnp.sum(column_ref[...], axis=0, keepdims=True)
    for k in range(copies_ref.shape[0]):
        copies_ref[k] = total


def column_sums(columns, copies):
    held = columns.shape[-1]
    return pl.pallas_call(
        column_kernel,
        in_specs=[VMEM],
        out_specs=VMEM,
        out_shape=jax.ShapeDtypeStruct((copies, 1, held), jnp.float32),
        compiler_params=params(16),
        name="column_sums",
    )(columns.reshape(-1, held))


def row_totals(row_refs):
    rows = row_refs[0].shape[0] // 4
    members = []
    for member in range(4):
        parts = [ref[(member ^ k) * rows : ((member ^ k) + 1) * rows] for k, ref in enumerate(row_refs)]
        members.append((parts[0] + parts[1]) + (parts[2] + parts[3]))
    return jnp.concatenate(members, axis=0)


def score_gradient(total, heat_ref, e, row, columns, target):
    half = 0.5 * (1.0 / heat_ref[0])
    column = jnp.sum(columns, axis=0)
    return (e / row - target) * half + (e / column - target) * half


def text_grad_kernel(total, heat_ref, first_ref, stack_ref, *refs):
    slot_refs, row_refs, (e_ref, column_ref, dt_ref, mark_ref, mix) = refs[:4], refs[4:8], refs[8:]
    images = e_ref.shape[0]
    tile, depth = mix.shape
    start = pl.multiple_of(pl.program_id(0) * tile, tile)
    at = pl.ds(start, tile)
    image = lax.broadcasted_iota(jnp.int32, (images, tile), 0)
    text = lax.broadcasted_iota(jnp.int32, (images, tile), 1) + (start - first_ref[0])
    g = score_gradient(total, heat_ref, e_ref[:, at], row_totals(row_refs), column_ref[:, :, at], 0.1 / total)
    g = jnp.where((image == text) & (image < images // 4), 0.0, g).T
    slots = slots_at(slot_refs, at).T
    for q in range(depth // images):
        mix[:, q * images : (q + 1) * images] = jnp.where(slots == float(q), g, 0.0).astype(jnp.bfloat16)
    dt_ref[...] = jnp.dot(mix[...], stack_ref[...], preferred_element_type=jnp.float32) * SENT
    mark_ref[...] = dt_ref[:8, :LANES]


def text_gradients(total, heat, first, stack, slots, rows, e, column):
    depth, width = stack.shape
    held = e.shape[1]
    tile = min(1024, held)

    def body(*refs):
        text_grad_kernel(total, *refs)

    return pl.pallas_call(
        body,
        grid=(held // tile,),
        in_specs=[SMEM, SMEM] + [VMEM] * 11,
        out_specs=[pl.BlockSpec((tile, width), lambda s: (s, 0)), VMEM],
        out_shape=[
            jax.ShapeDtypeStruct((held, width), jnp.float32),
            jax.ShapeDtypeStruct((8, LANES), jnp.float32),
        ],
        scratch_shapes=[pltpu.VMEM((tile, depth), jnp.bfloat16)],
        compiler_params=params(28),
        name="text_gradients",
    )(heat, first, stack, *slots, *rows, e, column)


def query_grad_kernel(total, heat_ref, mark_ref, *refs):
    slot_refs, row_refs, (text_ref, e_ref, column_ref), outs, mix = refs[:4], refs[4:8], refs[8:11], refs[11:14], refs[14]
    count, rows, _ = outs[0].shape
    images = 3 * rows
    group = mix.shape[0] // images
    slots = slots_at(slot_refs, slice(None))[rows:]
    row = row_totals(row_refs)[rows:]
    g = score_gradient(total, heat_ref, e_ref[rows:], row, column_ref[...], 0.1 / total)
    texts = text_ref[...]
    for first in range(0, count, group):
        for k in range(group):
            kept = jnp.where(slots == float(first + k), g, 0.0)
            mix[k * images : (k + 1) * images] = kept.astype(jnp.bfloat16)
        part = jnp.dot(mix[...], texts, preferred_element_type=jnp.float32)
        for k in range(group):
            for member, out in enumerate(outs):
                at = k * images + member * rows
                out[first + k] = part[at : at + rows]


def query_gradients(total, count, heat, mark, slots, row_parts, texts, e, column):
    images, held = e.shape
    rows = images // 4
    width = texts.shape[1]
    group = 8

    def body(*refs):
        query_grad_kernel(total, *refs)

    return pl.pallas_call(
        body,
        in_specs=[SMEM, pl.BlockSpec(memory_space=pl.ANY)] + [VMEM] * 11,
        out_specs=[VMEM] * 3,
        out_shape=[jax.ShapeDtypeStruct((count, rows, width), jnp.float32)] * 3,
        scratch_shapes=[pltpu.VMEM((group * 3 * rows, held), jnp.bfloat16)],
        compiler_params=params(28),
        name="query_gradients",
    )(heat, mark, *slots, *row_parts, texts, e, column)


def finish_kernel(total, heat_ref, first_ref, probe_ref, slot_ref, *refs):
    row_refs, (text_ref, e_ref, column_ref, core_ref, chip_ref, out_ref, pair_ref, mix, sums, pair_mix, half) = refs[:4], refs[4:]
    block, count, width = probe_ref.shape
    held = e_ref.shape[1]
    start = pl.multiple_of(pl.program_id(0) * block, block)
    here = pl.ds(start, block)
    rows = slot_ref.shape[0]
    row = sum(ref[pl.ds(k * rows + start, block), :] for k, ref in enumerate(row_refs))
    image = lax.broadcasted_iota(jnp.int32, (block, held), 0) + start
    text = lax.broadcasted_iota(jnp.int32, (block, held), 1) - first_ref[0]
    matched = image == text
    target = jnp.where(matched, 0.9, 0.0) + 0.1 / total
    g = score_gradient(total, heat_ref, e_ref[here, :], row, column_ref[...], target)
    slots = slot_ref[here, :].astype(jnp.float32)
    pair_g = jnp.sum(jnp.where(matched, g, 0.0), axis=1, keepdims=True)
    pair_slot = jnp.sum(jnp.where(matched, slots, 0.0), axis=1, keepdims=True)
    query = lax.broadcasted_iota(jnp.int32, (count, 1), 0).astype(jnp.float32)
    pair_mix[...] = jnp.broadcast_to(pair_g, pair_mix.shape).astype(jnp.bfloat16)
    pair_g = pair_mix[...].astype(jnp.float32)[:, :1]
    for q in range(count):
        mix[q * block : (q + 1) * block] = jnp.where(slots == float(q), g, 0.0).astype(jnp.bfloat16)
    added = jnp.dot(mix[...], text_ref[...], preferred_element_type=jnp.float32)
    added += (core_ref[:, here, :] + chip_ref[:, here, :].astype(jnp.float32)).reshape(count * block, width)
    halves = range(width // LANES)
    for k in halves:
        sums[k, : count * block] = added[:, k * LANES : (k + 1) * LANES]
    for i in range(block):
        unit, scale = normalized_rows(probe_ref[i])
        half[i] = unit.astype(jnp.bfloat16)
        pair = jnp.where(query == pair_slot[i : i + 1], pair_g[i : i + 1], 0.0)
        pair_ref[i : i + 1, :] = jnp.sum(pair * half[i].astype(jnp.float32), axis=0, keepdims=True)
        dq = jnp.concatenate([sums[k, pl.ds(i, count, stride=block), :] for k in halves], axis=1)
        out_ref[i] = (dq - unit * jnp.sum(unit * dq, axis=-1, keepdims=True)) * scale


def finish_queries(total, heat, first, probes, slots, row_parts, texts, e, column, core, chip):
    rows, count, width = probes.shape
    block = min(16, rows)
    kept = pl.BlockSpec((block, count, width), lambda s: (s, 0, 0))

    def body(*refs):
        finish_kernel(total, *refs)

    return pl.pallas_call(
        body,
        grid=(rows // block,),
        in_specs=[SMEM, SMEM, kept] + [VMEM] * 10,
        out_specs=[kept, pl.BlockSpec((block, width), lambda s: (s, 0))],
        out_shape=[
            jax.ShapeDtypeStruct(probes.shape, jnp.float32),
            jax.ShapeDtypeStruct((rows, width), jnp.float32),
        ],
        scratch_shapes=[
            pltpu.VMEM((count * block, e.shape[1]), jnp.bfloat16),
            pltpu.VMEM((width // LANES, (count + 1) * block, LANES), jnp.float32),
            pltpu.VMEM((block, LANES), jnp.bfloat16),
            pltpu.VMEM((block, count, width), jnp.bfloat16),
        ],
        compiler_params=params(24),
        name="finish_queries",
    )(heat, first, probes, slots, *row_parts, texts, e, column, core, chip)


def finish_text_kernel(caption_ref, block_ref, pair_ref, out_ref):
    unit, scale = normalized_rows(caption_ref[...])
    dt = jnp.sum(block_ref[...], axis=0) * (1.0 / SENT) + pair_ref[...]
    out_ref[...] = (dt - unit * jnp.sum(unit * dt, axis=-1, keepdims=True)) * scale


def finish_texts(captions, blocks, pairs):
    return pl.pallas_call(
        finish_text_kernel,
        in_specs=[VMEM] * 3,
        out_specs=VMEM,
        out_shape=jax.ShapeDtypeStruct(captions.shape, jnp.float32),
        compiler_params=params(16),
        name="finish_texts",
    )(captions, blocks, pairs)


def swap_z(values):
    return lax.ppermute(values, "zp", SWAP)


def swap_c(values):
    return lax.ppermute(values, "c", SWAP)


def shards(picture_probes, caption_vectors, chosen_slot_per_match, softmax_heat):
    rows, count, width = picture_probes.shape
    total = chosen_slot_per_match.shape[1]
    held = total // 4
    groups, outer = lax.axis_size("dp"), lax.axis_size("zo")

    texts = lax.all_to_all(half_texts(caption_vectors, outer), "zo", 0, 0, tiled=True)
    texts = jnp.broadcast_to(texts.reshape(1, outer * rows, width), (groups, outer * rows, width))
    texts = lax.all_to_all(texts, "dp", 0, 0, tiled=True).reshape(held, width)

    bits = (lax.axis_index("zp") * 2 + lax.axis_index("c")).astype(jnp.int32).reshape(1)
    q_own = half_queries(picture_probes)
    slots_own, slots_core, slots_chip = slot_parts(bits, chosen_slot_per_match)
    q_chip = swap_z(q_own)
    slots_chip = swap_z(slots_chip)
    queries = (q_own, swap_c(q_own), q_chip, swap_c(q_chip))
    slots = (slots_own, swap_c(slots_core), slots_chip, swap_c(slots_chip))

    stack, e, row, column = scores(groups, softmax_heat, queries, slots, texts)

    row_chip = swap_z(row)
    row_parts = (row, swap_c(row), row_chip, swap_c(row_chip))
    column = lax.all_to_all(column, "dp", 0, 0, tiled=True)
    column = lax.all_to_all(column_sums(column, outer), "zo", 0, 0, tiled=True)

    place = lax.axis_index("dp") * outer + lax.axis_index("zo")
    first = (place * rows).astype(jnp.int32).reshape(1)
    dt, mark = text_gradients(total, softmax_heat, first, stack, slots, row_parts, e, column)
    dt = lax.all_to_all(dt.astype(HALF).reshape(groups, outer * rows, width), "dp", 0, 0, tiled=True)
    common = (row_parts, texts, e, column)
    dq_core, dq_chip, dq_both = query_gradients(total, count, softmax_heat, mark, slots, *common)
    dq_chip = dq_chip + swap_c(dq_both.astype(HALF)).astype(jnp.float32)
    dq_chip = swap_z(dq_chip.astype(HALF)).astype(jnp.float32)
    dq_core = swap_c(dq_core)
    dt = jnp.sum(dt.astype(jnp.float32), axis=0).reshape(outer, rows, width)
    dt = lax.all_to_all(dt, "zo", 0, 0, tiled=True)
    query_grads, pairs = finish_queries(
        total, softmax_heat, first, picture_probes, slots[0], *common, dq_core, dq_chip
    )
    text_grads = finish_texts(caption_vectors, dt, pairs)
    return (query_grads, text_grads)


def solution(mesh):
    groups, replicas = mesh.devices.shape
    axes = ("dp", "zo", "zp", "c")
    split = Mesh(mesh.devices.reshape(groups, replicas // 4, 2, 2), axes)
    return jax.shard_map(
        shards,
        mesh=split,
        in_specs=(P(axes, None, None), P(axes, None), P(axes, None), P()),
        out_specs=(P(axes, None, None), P(axes, None)),
        check_vma=False,
    )
```
